32 devices in a mesh: groups: 2 (over y), hid: 8 (over z, x), row: 2 (over core).
Axes of the slice: x: 2, y: 2, z: 4, core: 2. Of those that a mesh axis runs over, the one named last changes fastest.
Arguments:
- gate_proj: bfloat16 [32, 32768], P(('groups', 'row'), 'hid'), parts along dimension 0, may hold values from -6 to 6
- up_proj: bfloat16 [32, 32768], P(('groups', 'row'), 'hid'), parts along dimension 0, may hold values from -6 to 6
- hadamard_signs: int32 [32768], P('hid'), may hold values from 0 to 1
- down_codes: bfloat16 [32768, 8192], P('hid', 'row'), may hold values from -127 to 127, as said below
- down_scales: int32 [8192], P('row'), may hold values from 128 to 1279
- residual: bfloat16 [32, 8192], P(('groups', 'hid'), 'row'), parts along dimension 0, may hold values from -16 to 16
- norm_gain: bfloat16 [8192], P('row'), may hold values from 0.099609375 to 1.8984375
- qkv_codes: bfloat16 [8192, 18432], P('row', 'hid'), may hold values from -127 to 127, as said below
- qkv_scales: int32 [18432], P('hid'), may hold values from 128 to 1279
Outputs:
- new_stream: bfloat16 [32, 8192], P(('groups', 'hid'), 'row'), parts along dimension 0
- joined_qkv: bfloat16 [32, 18432], P(('groups', 'row'), 'hid'), parts along dimension 0
The draws below stay inside these ranges and needn't reach their ends.
There are 2 independent parts, one for each index of `groups`. The reference program is written for one: setup_inputs(seed, part) draws one part's arguments, and reference() takes and returns one part's arrays. A program takes and returns all parts, laid end to end along the dimension named above; an argument that names none is the same for every part. Nothing has to cross between parts.
Inputs may be any that keep to these rules, and one draw needn't show every extreme that they name: `down_codes`: every entry is a whole number. `qkv_codes`: every entry is a whole number.
All inputs are finite; a program needn't handle non-finite values.
Results may differ from the reference program's by a relative error of at most 0.0062.
Values may be sent and summed in bfloat16 or wider, within the bound.
No kernel may reach another device: no remote copies, remote signals or barrier semaphores. Data moves between devices by JAX's collectives and lax.ppermute only.
A program may use at most 128 MiB of HBM per device.

```python
import math
import jax
import jax.numpy as jnp
from jax import lax

D = 8192
FF = 32768
QKV = 18432
ROWS = 16


def draw_down_codes(key, part):
    return jax.random.randint(jax.random.fold_in(key, 11), (FF, D), -127, 128).astype(jnp.float32).astype(jnp.bfloat16)


def draw_qkv_codes(key, part):
    return jax.random.randint(jax.random.fold_in(key, 23), (D, QKV), -127, 128).astype(jnp.float32).astype(jnp.bfloat16)


def draw_residual(key, part):
    base_key = jax.random.fold_in(key, 37)
    key_noise, key_column = jax.random.split(base_key, 2)
    column_rise = 0.3 * 3.0 ** (jnp.arange(D, dtype=jnp.float32) / D)
    column_spread = jnp.exp(jax.random.uniform(key_column, (D,), jnp.float32, 0.0, math.log(3.3)))
    noise_part = jax.random.truncated_normal(key_noise, -4.0, 4.0, (ROWS, D), jnp.float32)
    values = noise_part * (column_rise * column_spread)[None, :]
    return jnp.clip(values, -16.0, 16.0).astype(jnp.bfloat16)


def place_ends(array, key, smallest, largest):
    place = [jax.random.randint(jax.random.fold_in(key, axis), (), 0, length) for axis, length in enumerate(array.shape)]
    main_axis = array.shape.index(max(array.shape))
    neighbour = place[:main_axis] + [(place[main_axis] + 1) % array.shape[main_axis]] + place[main_axis + 1:]
    return array.at[tuple(place)].set(smallest).at[tuple(neighbour)].set(largest)


def steps_of(own_key, dims, cuts, low, top_value):
    gain = 1.0
    for axis_at, shards_of in cuts:
        steps = jax.random.uniform(jax.random.fold_in(jax.random.fold_in(own_key, 6), axis_at), (shards_of,), jnp.float32, low / len(cuts), top_value / len(cuts))
        gain = gain * jnp.repeat(jnp.exp(steps), dims[axis_at] // shards_of).reshape((-1,) + (1,) * (len(dims) - 1 - axis_at))
    return gain


def normal_values(stream_key, shape, spread, limit, shards=(), held_as=jnp.bfloat16):
    values = jax.random.normal(stream_key, shape, jnp.float32) * spread
    if len(shards) > 0:
        values = steps_of(stream_key, shape, shards, -0.22, 0.18) * values
    return jnp.clip(values, min=-limit, max=limit).astype(held_as)


def setup_inputs(seed: int = 0, part: int = 0) -> dict:
    arg_keys = jax.random.split(jax.random.key(seed), 10)
    part_splits = jax.random.split(jax.random.fold_in(arg_keys[9], part), 10)
    gate_proj = normal_values(part_splits[0], (ROWS, FF), 1.0, 6.0, ((0, 2), (1, 8)))
    up_proj = normal_values(part_splits[1], (ROWS, FF), 1.0, 6.0, ((0, 2), (1, 8)))
    hadamard_signs = place_ends(jax.random.randint(arg_keys[2], (FF,), 0, 2), jax.random.fold_in(arg_keys[2], 1), 0, 1).astype(jnp.int32)
    down_codes = draw_down_codes(jax.random.fold_in(arg_keys[9], 71), part)
    down_scales = place_ends(jax.random.randint(arg_keys[4], (D,), 128, 1280), jax.random.fold_in(arg_keys[4], 1), 128, 1279).astype(jnp.int32)
    residual = draw_residual(jax.random.fold_in(jax.random.fold_in(arg_keys[9], part), 71), part)
    norm_gain = jnp.clip(1.0 + 0.18 * jax.random.normal(arg_keys[6], (D,), jnp.float32), 0.099609375, 1.8984375).astype(jnp.bfloat16)
    qkv_codes = draw_qkv_codes(jax.random.fold_in(arg_keys[9], 71), part)
    qkv_scales = place_ends(jax.random.randint(arg_keys[8], (QKV,), 128, 1280), jax.random.fold_in(arg_keys[8], 1), 128, 1279).astype(jnp.int32)
    return {"gate_proj": gate_proj, "up_proj": up_proj, "hadamard_signs": hadamard_signs, "down_codes": down_codes, "down_scales": down_scales, "residual": residual, "norm_gain": norm_gain, "qkv_codes": qkv_codes, "qkv_scales": qkv_scales}


def sylvester(order_size):
    row_index = lax.broadcasted_iota(jnp.int32, (order_size, order_size), 0)
    column_index = lax.broadcasted_iota(jnp.int32, (order_size, order_size), 1)
    result = jnp.ones((order_size, order_size), jnp.float32)
    for bit_number in range(order_size.bit_length() - 1):
        both_set = row_index // 2 ** bit_number % 2 * (column_index // 2 ** bit_number % 2)
        result = result * (1.0 - 2.0 * both_set.astype(jnp.float32))
    return result

def factor_list(length):
    factors = []
    remain = length
    while remain > 1:
        factor = min(remain, 128)
        factors.append(factor)
        remain = remain // factor
    return factors

def transform_axis(values, order_size, axis_place):
    if order_size == 1:
        return values
    product_moved = jnp.tensordot(values, sylvester(order_size), axes=([axis_place], [0]), precision=lax.Precision.HIGHEST)
    return jnp.moveaxis(product_moved, -1, axis_place)

def transform_last(values):
    factors = factor_list(values.shape[-1])
    leading = values.shape[:-1]
    shaped = values.reshape(leading + tuple(factors))
    for offset, order_size in enumerate(factors):
        shaped = transform_axis(shaped, order_size, len(leading) + offset)
    return shaped.reshape(values.shape)

def reference(gate_proj, up_proj, hadamard_signs, down_codes, down_scales, residual, norm_gain, qkv_codes, qkv_scales):
    hidden = (jax.nn.silu(gate_proj.astype(jnp.float32)) * up_proj.astype(jnp.float32)).astype(jnp.bfloat16)
    flips = (1 - 2 * hadamard_signs).astype(jnp.bfloat16)
    signed = hidden * flips[None, :]
    rotated = (transform_last(signed.astype(jnp.float32)) * (1.0 / math.sqrt(FF))).astype(jnp.bfloat16)
    down = jnp.dot(rotated, down_codes, preferred_element_type=jnp.float32)
    down = down * (down_scales.astype(jnp.float32) * 2.0 ** (-23))[None, :]
    new_stream = (residual.astype(jnp.float32) + down).astype(jnp.bfloat16)
    stream_wide = new_stream.astype(jnp.float32)
    squares = lax.optimization_barrier(jnp.sum(stream_wide * stream_wide, axis=1))
    scaled_rows = (stream_wide * norm_gain.astype(jnp.float32)[None, :]).astype(jnp.bfloat16)
    projected = jnp.dot(scaled_rows, qkv_codes, preferred_element_type=jnp.float32)
    inverse = lax.rsqrt(squares / D + 1e-05)
    joined_qkv = (projected * inverse[:, None] * (qkv_scales.astype(jnp.float32) * 2.0 ** (-22))[None, :]).astype(jnp.bfloat16)
    return (new_stream, joined_qkv)
```

```python
import math

import jax
import jax.numpy as jnp
from jax import lax
from jax.experimental import pallas as pl
from jax.experimental.pallas import tpu as pltpu
from jax.sharding import PartitionSpec as P

epsilon = 1e-05
lanes = 128
VMEM = pl.BlockSpec(memory_space=pltpu.VMEM)
f32, bf16 = jnp.float32, jnp.bfloat16


def exchange(block, axis, distance):
    count = lax.axis_size(axis)
    return lax.ppermute(block, axis, [(i, i ^ distance) for i in range(count)])


def bit_of(axis, distance):
    return lax.axis_index(axis) // distance % 2


def params(mib):
    return pltpu.CompilerParams(vmem_limit_bytes=mib << 20)


def cost(flops, nbytes):
    return pl.CostEstimate(flops=flops, bytes_accessed=nbytes, transcendentals=0)


def tile_of(width):
    return 256 if width % 256 == 0 else 128


def signed_kernel(gate_ref, up_ref, sign_ref, out_ref):
    gate = gate_ref[...].astype(f32)
    hidden = (gate / (1.0 + jnp.exp(-gate)) * up_ref[...].astype(f32)).astype(bf16)
    flips = (1 - 2 * sign_ref[...]).astype(f32)
    out_ref[...] = (hidden.astype(f32) * flips).astype(bf16)


def signed_units(gate, up, signs):
    return pl.pallas_call(
        signed_kernel,
        out_shape=jax.ShapeDtypeStruct(gate.shape, bf16),
        in_specs=[VMEM] * 3,
        out_specs=VMEM,
        compiler_params=params(4),
        cost_estimate=cost(0, 40 << 20),
        name="signed_units",
    )(gate, up, signs.reshape(1, -1))


def hadamard_128():
    both = lax.broadcasted_iota(jnp.int32, (lanes, lanes), 0) & lax.broadcasted_iota(
        jnp.int32, (lanes, lanes), 1
    )
    for shift in (4, 2, 1):
        both = both ^ (both >> shift)
    return (1 - 2 * (both & 1)).astype(f32).astype(bf16)


def mix_kernel(own_ref, other_ref, wide_ref, send_ref):
    rows, width = own_ref.shape
    matrix = hadamard_128()
    upper = bit_of("hid", 1) == 1
    own, other = own_ref[...].astype(f32), other_ref[...].astype(f32)
    stacked = jnp.concatenate([other, own], axis=0).astype(bf16)
    blocks = []
    for j in range(width // lanes):
        product = jnp.dot(
            stacked[:, j * lanes : (j + 1) * lanes], matrix, preferred_element_type=f32
        )
        theirs, mine = product[:rows], product[rows:]
        blocks.append(theirs + jnp.where(upper, -mine, mine))
    step = 1
    while step < len(blocks):
        for j in range(len(blocks)):
            if not j & step:
                a, b = blocks[j], blocks[j | step]
                blocks[j], blocks[j | step] = a + b, a - b
        step *= 2
    for j, block in enumerate(blocks):
        wide_ref[:, j * lanes : (j + 1) * lanes] = block
        send_ref[:, j * lanes : (j + 1) * lanes] = block.astype(bf16)


def mix(own, other):
    return pl.pallas_call(
        mix_kernel,
        out_shape=(jax.ShapeDtypeStruct(own.shape, f32), jax.ShapeDtypeStruct(own.shape, bf16)),
        in_specs=[VMEM] * 2,
        out_specs=(VMEM, VMEM),
        compiler_params=params(4),
        name="mix",
    )(own, other)


def down_half(rows, weight, scale, placed, other_half):
    count, depth = rows.shape
    half = weight.shape[1] // 2
    bn = tile_of(half)

    def kernel(x_ref, w_ref, s_ref, p_ref, o_ref):
        side = bit_of("hid", 1)
        if other_half:
            side = 1 - side

        @pl.loop(0, half // bn)
        def _(n):
            at = pl.multiple_of(n * bn, bn)
            there = pl.ds(pl.multiple_of(side * half + at, bn), bn)
            total = jnp.dot(x_ref[...], w_ref[:, there], preferred_element_type=f32)
            o_ref[:, pl.ds(at, bn)] = total * (s_ref[:, there].astype(f32) * 2.0 ** (-23)) + p_ref[:, there]

    return pl.pallas_call(
        kernel,
        out_shape=jax.ShapeDtypeStruct((count, half), f32),
        in_specs=[VMEM] * 4,
        out_specs=VMEM,
        compiler_params=params(4),
        cost_estimate=cost(2 * count * depth * half, 2 * depth * half),
        name="down_other" if other_half else "down_own",
    )(rows, weight, scale, placed)


def qkv_half(stream, gain, weight, before, own_half):
    count, depth = stream.shape
    width = weight.shape[1]
    bn = tile_of(width)

    def kernel(x_ref, g_ref, w_ref, *refs):
        if own_half:
            o_ref, q_ref, scaled = refs
        else:
            before_ref, squares_ref, o_ref, q_ref, scaled = refs
        side = bit_of("hid", 1)
        if not own_half:
            side = 1 - side
        there = pl.ds(pl.multiple_of(side * depth, depth), depth)
        wide = x_ref[...].astype(f32)
        scaled[...] = (wide * g_ref[:, there].astype(f32)).astype(bf16)
        squares = jnp.broadcast_to(jnp.sum(wide * wide, axis=1, keepdims=True), q_ref.shape)
        if not own_half:
            squares = squares + squares_ref[...]
        q_ref[...] = squares

        @pl.loop(0, width // bn)
        def _(n):
            columns = pl.ds(pl.multiple_of(n * bn, bn), bn)
            total = jnp.dot(scaled[...], w_ref[there, columns], preferred_element_type=f32)
            if not own_half:
                total += before_ref[:, columns]
            o_ref[:, columns] = total

    return pl.pallas_call(
        kernel,
        out_shape=(
            jax.ShapeDtypeStruct((count, width), f32),
            jax.ShapeDtypeStruct((count, lanes), f32),
        ),
        in_specs=[VMEM] * (3 + len(before)),
        out_specs=(VMEM, VMEM),
        scratch_shapes=[pltpu.VMEM((count, depth), bf16)],
        compiler_params=params(4),
        cost_estimate=cost(2 * count * depth * width, 2 * depth * width),
        name="qkv_own" if own_half else "qkv_other",
    )(stream, gain, weight, *before)


def body(
    gate_proj,
    up_proj,
    hadamard_signs,
    down_codes,
    down_scales,
    residual,
    norm_gain,
    qkv_codes,
    qkv_scales,
):
    hid, n_row = lax.axis_size("hid"), lax.axis_size("row")
    me_hid, me_row = lax.axis_index("hid"), lax.axis_index("row")
    own_rows, depth = gate_proj.shape
    all_rows = own_rows * n_row
    res_rows, features = residual.shape
    half = features // 2
    distances = [1 << b for b in range(hid.bit_length() - 1)]

    def natural(block):
        return block ^ me_row

    spot = lax.broadcasted_iota(jnp.int32, (all_rows, 1), 0)
    spot = natural(spot // own_rows) * own_rows + spot % own_rows - me_hid * res_rows
    placed = jnp.zeros((all_rows, features), f32)
    for r in range(res_rows):
        placed = jnp.where(spot == r, residual[r : r + 1].astype(f32), placed)

    down_codes = pltpu.with_memory_space_constraint(down_codes, pltpu.VMEM)
    qkv_codes = pltpu.with_memory_space_constraint(qkv_codes, pltpu.VMEM)

    signed = signed_units(gate_proj, up_proj, hadamard_signs)
    send = signed
    for k, distance in enumerate(distances):
        other = exchange(send, "hid", distance)
        if k == 0:
            wide, send = mix(signed, other)
        else:
            upper = bit_of("hid", distance) == 1
            wide = other.astype(f32) + jnp.where(upper, -wide, wide)
            send = wide.astype(bf16)
    rotated = (wide * (1.0 / math.sqrt(depth * hid))).astype(bf16)
    rows = [rotated] + [exchange(rotated, "row", j) for j in range(1, n_row)]
    rows = jnp.concatenate(rows, axis=0)

    scale = down_scales.reshape(1, -1)
    theirs = down_half(rows, down_codes, scale, placed, True)
    arrived = exchange(theirs, "hid", 1)
    total = down_half(rows, down_codes, scale, placed, False) + arrived
    for distance in distances[1:]:
        total = total + exchange(total.astype(bf16), "hid", distance).astype(f32)
    stream = total.astype(bf16)
    stream_other = exchange(stream, "hid", 1)

    gain = norm_gain.reshape(1, -1)
    part = qkv_half(stream, gain, qkv_codes, (), True)
    projected, squares = qkv_half(stream_other, gain, qkv_codes, part, False)
    both = jnp.concatenate([projected, squares], axis=1)
    mine = both[:own_rows]
    for j in range(1, n_row):
        mine = mine + exchange(both[j * own_rows : (j + 1) * own_rows], "row", j)
    width = projected.shape[1]
    inverse = lax.rsqrt(mine[:, width : width + 1] / (features * n_row) + epsilon)
    joined_qkv = (mine[:, :width] * inverse * (qkv_scales.astype(f32) * 2.0 ** (-22))[None, :]).astype(bf16)

    lower = bit_of("hid", 1) == 0
    full = jnp.concatenate(
        [jnp.where(lower, stream, stream_other), jnp.where(lower, stream_other, stream)], axis=1
    )
    first = me_hid * res_rows
    first = natural(first // own_rows) * own_rows + first % own_rows
    new_stream = lax.dynamic_slice_in_dim(full, first, res_rows, 0)
    return (new_stream, joined_qkv)


def solution(mesh):
    return jax.shard_map(
        body,
        mesh=mesh,
        in_specs=(
            P(("groups", "row"), "hid"),
            P(("groups", "row"), "hid"),
            P("hid"),
            P("hid", "row"),
            P("row"),
            P(("groups", "hid"), "row"),
            P("row"),
            P("row", "hid"),
            P("hid"),
        ),
        out_specs=(P(("groups", "hid"), "row"), P(("groups", "row"), "hid")),
        check_vma=False,
    )
```

```python
import math

import jax
import jax.numpy as jnp
from jax import lax
from jax.experimental import pallas as pl
from jax.experimental.pallas import tpu as pltpu
from jax.sharding import PartitionSpec as P

epsilon = 1e-05
lanes = 128
VMEM = pl.BlockSpec(memory_space=pltpu.VMEM)
HBM = pl.BlockSpec(memory_space=pltpu.HBM)
f32, bf16 = jnp.float32, jnp.bfloat16


def exchange(block, axis, distance):
    count = lax.axis_size(axis)
    return lax.ppermute(block, axis, [(i, i ^ distance) for i in range(count)])


def bit_of(axis, distance):
    return lax.axis_index(axis) // distance % 2


def in_hbm(array):
    return pltpu.with_memory_space_constraint(array, pltpu.HBM)


def in_vmem(array):
    return pltpu.with_memory_space_constraint(array, pltpu.VMEM)


def params(mib):
    return pltpu.CompilerParams(vmem_limit_bytes=mib << 20)


def cost(flops, nbytes):
    return pl.CostEstimate(flops=flops, bytes_accessed=nbytes, transcendentals=0)


def tile_of(width):
    parts = next(p for p in (1, 2, 3, 4, 6, 8, 9, 12) if width // p <= 1152 and width % (p * lanes) == 0)
    return width // parts


def signed_kernel(gate_hbm, up_hbm, sign_hbm, out_ref, gate_ref, up_ref, sign_ref, sems):
    copies = [
        pltpu.make_async_copy(gate_hbm, gate_ref, sems.at[0]),
        pltpu.make_async_copy(up_hbm, up_ref, sems.at[1]),
        pltpu.make_async_copy(sign_hbm, sign_ref, sems.at[2]),
    ]
    for copy in copies:
        copy.start()
    for copy in copies:
        copy.wait()
    gate = gate_ref[...].astype(f32)
    hidden = (gate / (1.0 + jnp.exp(-gate)) * up_ref[...].astype(f32)).astype(bf16)
    flips = (1 - 2 * sign_ref[...]).astype(f32)
    out_ref[...] = (hidden.astype(f32) * flips).astype(bf16)


def signed_units(gate, up, signs):
    signs = signs.reshape(1, -1)
    return pl.pallas_call(
        signed_kernel,
        out_shape=jax.ShapeDtypeStruct(gate.shape, bf16),
        in_specs=[HBM] * 3,
        out_specs=VMEM,
        scratch_shapes=[
            pltpu.VMEM(gate.shape, bf16),
            pltpu.VMEM(gate.shape, bf16),
            pltpu.VMEM(signs.shape, jnp.int32),
            pltpu.SemaphoreType.DMA((3,)),
        ],
        compiler_params=params(4),
        name="signed_units",
    )(in_hbm(gate), in_hbm(up), in_hbm(signs))


def hadamard_128():
    both = lax.broadcasted_iota(jnp.int32, (lanes, lanes), 0) & lax.broadcasted_iota(
        jnp.int32, (lanes, lanes), 1
    )
    for shift in (4, 2, 1):
        both = both ^ (both >> shift)
    return (1 - 2 * (both & 1)).astype(f32).astype(bf16)


def mix_kernel(own_ref, other_ref, wide_ref, send_ref):
    rows, width = own_ref.shape
    matrix = hadamard_128()
    upper = bit_of("hid", 1) == 1
    own, other = own_ref[...].astype(f32), other_ref[...].astype(f32)
    stacked = jnp.concatenate([other, own], axis=0).astype(bf16)
    blocks = []
    for j in range(width // lanes):
        product = jnp.dot(
            stacked[:, j * lanes : (j + 1) * lanes], matrix, preferred_element_type=f32
        )
        theirs, mine = product[:rows], product[rows:]
        blocks.append(theirs + jnp.where(upper, -mine, mine))
    step = 1
    while step < len(blocks):
        for j in range(len(blocks)):
            if not j & step:
                a, b = blocks[j], blocks[j | step]
                blocks[j], blocks[j | step] = a + b, a - b
        step *= 2
    for j, block in enumerate(blocks):
        wide_ref[:, j * lanes : (j + 1) * lanes] = block
        send_ref[:, j * lanes : (j + 1) * lanes] = block.astype(bf16)


def mix(own, other):
    return pl.pallas_call(
        mix_kernel,
        out_shape=(jax.ShapeDtypeStruct(own.shape, f32), jax.ShapeDtypeStruct(own.shape, bf16)),
        in_specs=[VMEM] * 2,
        out_specs=(VMEM, VMEM),
        compiler_params=params(4),
        name="mix",
    )(own, other)


def combine(wide, other, distance, factor):
    def kernel(wide_ref, other_ref, *out_refs):
        own, theirs = wide_ref[...], other_ref[...].astype(f32)
        mixed = theirs + jnp.where(bit_of("hid", distance) == 1, -own, own)
        if factor is None:
            out_refs[0][...] = mixed
            out_refs[1][...] = mixed.astype(bf16)
        else:
            out_refs[0][...] = (mixed * factor).astype(bf16)

    types = (f32, bf16) if factor is None else (bf16,)
    return pl.pallas_call(
        kernel,
        out_shape=tuple(jax.ShapeDtypeStruct(wide.shape, t) for t in types),
        in_specs=[VMEM] * 2,
        out_specs=(VMEM,) * len(types),
        compiler_params=params(4),
        name="combine",
    )(wide, other)


def add(total, arrived, last, first):
    def kernel(total_ref, arrived_ref, *out_refs):
        value = total_ref[...] + arrived_ref[...].astype(f32)
        if not last:
            out_refs[0][...] = value
        out_refs[-1][...] = value.astype(bf16)

    types = (bf16,) if last else (f32, bf16)
    return pl.pallas_call(
        kernel,
        out_shape=tuple(jax.ShapeDtypeStruct(total.shape, t) for t in types),
        in_specs=[VMEM] * 2,
        out_specs=(VMEM,) * len(types),
        compiler_params=params(4),
        cost_estimate=cost(40_000_000_000, 0) if not last else None,
        name="add",
    )(total, arrived)


def places(res_rows, own_rows):
    first, me_row = lax.axis_index("hid") * res_rows, lax.axis_index("row")
    found = []
    for r in range(res_rows):
        row = first + r
        found.append(((row // own_rows) ^ me_row) * own_rows + row % own_rows)
    return found


def half_columns(weight_ref, start, count, other_half):
    half = weight_ref.shape[1] // 2
    side = bit_of("hid", 1)
    if other_half:
        side = 1 - side
    return weight_ref.at[pl.ds(start, count), pl.ds(pl.multiple_of(side * half, half), half)]


def load_rows(weight, start, count, other_half, after):
    def kernel(after_ref, weight_ref, out_ref, sem):
        copy = pltpu.make_async_copy(half_columns(weight_ref, start, count, other_half), out_ref, sem)
        copy.start()
        copy.wait()

    return pl.pallas_call(
        kernel,
        out_shape=pltpu.VMEM((count, weight.shape[1] // 2), weight.dtype),
        in_specs=[VMEM, HBM],
        out_specs=VMEM,
        scratch_shapes=[pltpu.SemaphoreType.DMA],
        compiler_params=params(2),
        cost_estimate=cost(0, count * weight.shape[1]),
        name="load_rows",
    )(after, in_hbm(weight))


def tie(first, second):
    return lax.optimization_barrier((first, second))


def down_half(rows, chunks, weight, scale, residual, own_rows, other_half, ahead):
    count, depth = rows.shape
    half = weight.shape[1] // 2
    bn = tile_of(half)
    n_chunks = len(chunks)
    starts = [sum(c.shape[0] for c in chunks[:i]) for i in range(n_chunks + 1)]
    loaded = starts[-1]
    rest = depth - loaded
    pieces = max(p for p in (1, 2, 3, 4, 5, 6) if rest % (p * lanes) == 0) if rest else 0
    piece = rest // max(pieces, 1)
    first, few = ahead

    def kernel(x_ref, *refs):
        refs = list(refs)
        chunk_refs = [refs.pop(0) for _ in range(n_chunks)]
        w_ref, s_ref, r_ref, o_ref = (refs.pop(0) for _ in range(4))
        if few:
            ahead_ref = refs.pop(0)
        if rest:
            buf = refs.pop(0)
        sems = refs.pop(0)
        copies = [
            pltpu.make_async_copy(
                half_columns(w_ref, loaded + i * piece, piece, other_half),
                buf.at[pl.ds(i * piece, piece)],
                sems.at[i],
            )
            for i in range(pieces)
        ]
        if few:
            copies.append(
                pltpu.make_async_copy(
                    half_columns(w_ref, first, few, not other_half), ahead_ref, sems.at[pieces]
                )
            )
        for copy in copies:
            copy.start()
        side = bit_of("hid", 1)
        if other_half:
            side = 1 - side
        where = places(r_ref.shape[0], own_rows)
        index = lax.broadcasted_iota(jnp.int32, (count, bn), 0)
        parts = [(refs_at, start, ref.shape[0]) for refs_at, (start, ref) in enumerate(zip(starts, chunk_refs))]
        steps = [[(chunk_refs[i], start, 0, size) for i, start, size in parts]] if parts else []
        for i in range(pieces):
            steps.append([(buf, loaded + i * piece, i * piece, piece)])

        for i, step in enumerate(steps):
            if parts and i > 0:
                copies[i - 1].wait()
            elif not parts:
                copies[i].wait()

            @pl.loop(0, half // bn)
            def _(n):
                here = pl.ds(pl.multiple_of(n * bn, lanes), bn)
                total = jnp.zeros((count, bn), f32) if i == 0 else o_ref[:, here]
                for ref, x_at, at, size in step:
                    total += jnp.dot(
                        x_ref[:, x_at : x_at + size],
                        ref[at : at + size, here],
                        preferred_element_type=f32,
                    )
                if i == len(steps) - 1:
                    there = pl.ds(pl.multiple_of(side * half + n * bn, lanes), bn)
                    total = total * (s_ref[:, there].astype(f32) * 2.0 ** (-23))
                    residual_rows = r_ref[:, there].astype(f32)
                    for r, place in enumerate(where):
                        total = total + jnp.where(index == place, residual_rows[r : r + 1], 0.0)
                o_ref[:, here] = total

        if few:
            copies[-1].wait()

    out_shape = [jax.ShapeDtypeStruct((count, half), f32)]
    scratch = [pltpu.SemaphoreType.DMA((pieces + 1,))]
    if few:
        out_shape.append(pltpu.VMEM((few, half), weight.dtype))
    if rest:
        scratch.insert(0, pltpu.VMEM((rest, half), bf16))
    return pl.pallas_call(
        kernel,
        out_shape=tuple(out_shape),
        in_specs=[VMEM] * (1 + n_chunks) + [HBM, VMEM, VMEM],
        out_specs=(VMEM,) * len(out_shape),
        scratch_shapes=scratch,
        compiler_params=params(14),
        cost_estimate=cost(2 * count * depth * half, 2 * depth * half),
        name="down_other" if other_half else "down_own",
    )(rows, *map(in_vmem, chunks), in_hbm(weight), scale, residual)


def qkv_half(stream, gain, weight, before, own_rows):
    count, depth = stream.shape
    width = weight.shape[1]
    bn = tile_of(width)
    own_half = before is None
    first_rows = [(0, count)] if own_half else [(0, own_rows), (own_rows, count - own_rows)]

    def kernel(x_ref, g_ref, w_ref, *refs):
        before_ref = None if own_half else refs[0]
        out_refs, scaled = refs[-1 - len(first_rows) : -1], refs[-1]
        side = bit_of("hid", 1)
        if not own_half:
            side = 1 - side
        there = pl.ds(pl.multiple_of(side * depth, depth), depth)
        wide = x_ref[...].astype(f32)
        scaled[...] = (wide * g_ref[:, there].astype(f32)).astype(bf16)
        squares = jnp.broadcast_to(jnp.sum(wide * wide, axis=1, keepdims=True), (count, lanes))

        def put(columns, value):
            if not own_half:
                value = value + before_ref[:, columns]
            for ref, (start, size) in zip(out_refs, first_rows):
                ref[:, columns] = value[start : start + size]

        put(pl.ds(width, lanes), squares)

        for n in range(width // bn):
            columns = pl.ds(n * bn, bn)
            put(columns, jnp.dot(scaled[...], w_ref[there, columns], preferred_element_type=f32))

    operands = (stream, gain, weight) + (() if own_half else (before,))
    return pl.pallas_call(
        kernel,
        out_shape=tuple(jax.ShapeDtypeStruct((size, width + lanes), f32) for _, size in first_rows),
        in_specs=[VMEM] * len(operands),
        out_specs=(VMEM,) * len(first_rows),
        scratch_shapes=[pltpu.VMEM((count, depth), bf16)],
        compiler_params=params(4),
        cost_estimate=cost(2 * count * depth * width, 2 * depth * width),
        name="qkv_own" if own_half else "qkv_other",
    )(*operands)


def take_rows(stream, stream_other, res_rows, own_rows):
    count, half = stream.shape

    def kernel(own_ref, other_ref, out_ref):
        index = lax.broadcasted_iota(jnp.int32, (count, half), 0)
        side = bit_of("hid", 1)
        for ref, at in ((own_ref, side), (other_ref, 1 - side)):
            wide = ref[...].astype(f32)
            taken = [
                jnp.sum(jnp.where(index == place, wide, 0.0), axis=0, keepdims=True)
                for place in places(res_rows, own_rows)
            ]
            there = pl.ds(pl.multiple_of(at * half, half), half)
            out_ref[:, there] = jnp.concatenate(taken, axis=0).astype(bf16)

    return pl.pallas_call(
        kernel,
        out_shape=jax.ShapeDtypeStruct((res_rows, 2 * half), bf16),
        in_specs=[VMEM] * 2,
        out_specs=VMEM,
        compiler_params=params(4),
        name="take_rows",
    )(stream, stream_other)


def body(
    gate_proj,
    up_proj,
    hadamard_signs,
    down_codes,
    down_scales,
    residual,
    norm_gain,
    qkv_codes,
    qkv_scales,
):
    hid, n_row = lax.axis_size("hid"), lax.axis_size("row")
    own_rows, depth = gate_proj.shape
    res_rows, features = residual.shape
    distances = [1 << b for b in range(hid.bit_length() - 1)]

    send = signed_units(gate_proj, up_proj, hadamard_signs)
    chunks, loaded = [], 0
    share = -(-depth // len(distances) // lanes) * lanes
    for k, distance in enumerate(distances):
        other = exchange(send, "hid", distance)
        count = min(share, depth - loaded)
        chunk = load_rows(down_codes, loaded, count, True, send)
        other, chunk = tie(other, chunk)
        chunks.append(chunk)
        loaded += count
        last = k == len(distances) - 1
        if k == 0:
            wide, send = mix(send, other)
        elif not last:
            wide, send = combine(wide, other, distance, None)
        else:
            (rotated,) = combine(wide, other, distance, 1.0 / math.sqrt(depth * hid))
    rows = [rotated] + [exchange(rotated, "row", j) for j in range(1, n_row)]
    early = depth * 3 // 32 // lanes * lanes
    own_chunk = load_rows(down_codes, 0, early, False, rotated)
    rows[-1], own_chunk = tie(rows[-1], own_chunk)
    rows = jnp.concatenate(rows, axis=0)

    scale = down_scales.reshape(1, -1)
    ahead = (early, depth * 11 // 32 // lanes * lanes)
    theirs, next_chunk = down_half(rows, chunks, down_codes, scale, residual, own_rows, True, ahead)
    arrived = exchange(theirs, "hid", 1)
    own_chunks = [own_chunk, next_chunk]
    (total,) = down_half(rows, own_chunks, down_codes, scale, residual, own_rows, False, (0, 0))
    for distance in distances[1:]:
        total, send = add(total, arrived, False, distance == 2)
        arrived = exchange(send, "hid", distance)
    (stream,) = add(total, arrived, True, False)
    stream_other = exchange(stream, "hid", 1)

    gain = norm_gain.reshape(1, -1)
    (part,) = qkv_half(stream, gain, qkv_codes, None, own_rows)
    mine, rest = qkv_half(stream_other, gain, qkv_codes, part, own_rows)
    for j in range(1, n_row):
        mine = mine + exchange(rest[(j - 1) * own_rows : j * own_rows], "row", j)
    width = qkv_codes.shape[1]
    inverse = lax.rsqrt(mine[:, width : width + 1] / (features * n_row) + epsilon)
    joined_qkv = (mine[:, :width] * inverse * (qkv_scales.astype(f32) * 2.0 ** (-22))[None, :]).astype(bf16)
    return (take_rows(stream, stream_other, res_rows, own_rows), joined_qkv)


def solution(mesh):
    return jax.shard_map(
        body,
        mesh=mesh,
        in_specs=(
            P(("groups", "row"), "hid"),
            P(("groups", "row"), "hid"),
            P("hid"),
            P("hid", "row"),
            P("row"),
            P(("groups", "hid"), "row"),
            P("row"),
            P("row", "hid"),
            P("hid"),
        ),
        out_specs=(P(("groups", "hid"), "row"), P(("groups", "row"), "hid")),
        check_vma=False,
    )
```

```python
import math

import jax
import jax.numpy as jnp
from jax import lax
from jax.experimental import pallas as pl
from jax.experimental.pallas import tpu as pltpu
from jax.sharding import PartitionSpec as P

epsilon = 1e-05
lanes = 128
VMEM = pl.BlockSpec(memory_space=pltpu.VMEM)
HBM = pl.BlockSpec(memory_space=pltpu.HBM)
f32, bf16 = jnp.float32, jnp.bfloat16


def exchange(block, axis, distance):
    count = lax.axis_size(axis)
    return lax.ppermute(block, axis, [(i, i ^ distance) for i in range(count)])


def bit_of(axis, distance):
    return lax.axis_index(axis) // distance % 2


def in_hbm(array):
    return pltpu.with_memory_space_constraint(array, pltpu.HBM)


def in_vmem(array):
    return pltpu.with_memory_space_constraint(array, pltpu.VMEM)


def params(mib, rows=16):
    return pltpu.CompilerParams(vmem_limit_bytes=mib * max(1, rows // 16) << 20)


def cost(flops, nbytes):
    return pl.CostEstimate(flops=flops, bytes_accessed=nbytes, transcendentals=0)


def tile_of(width):
    parts = next(p for p in (1, 2, 3, 4, 6, 8, 9, 12) if width // p <= 1152 and width % (p * lanes) == 0)
    return width // parts


def signed_kernel(gate_hbm, up_hbm, sign_hbm, out_ref, gate_ref, up_ref, sign_ref, sems):
    copies = [
        pltpu.make_async_copy(gate_hbm, gate_ref, sems.at[0]),
        pltpu.make_async_copy(up_hbm, up_ref, sems.at[1]),
        pltpu.make_async_copy(sign_hbm, sign_ref, sems.at[2]),
    ]
    for copy in copies:
        copy.start()
    for copy in copies:
        copy.wait()
    gate = gate_ref[...].astype(f32)
    hidden = (gate / (1.0 + jnp.exp(-gate)) * up_ref[...].astype(f32)).astype(bf16)
    flips = (1 - 2 * sign_ref[...]).astype(f32)
    out_ref[...] = (hidden.astype(f32) * flips).astype(bf16)


def signed_units(gate, up, signs):
    signs = signs.reshape(1, -1)
    return pl.pallas_call(
        signed_kernel,
        out_shape=jax.ShapeDtypeStruct(gate.shape, bf16),
        in_specs=[HBM] * 3,
        out_specs=VMEM,
        scratch_shapes=[
            pltpu.VMEM(gate.shape, bf16),
            pltpu.VMEM(gate.shape, bf16),
            pltpu.VMEM(signs.shape, jnp.int32),
            pltpu.SemaphoreType.DMA((3,)),
        ],
        compiler_params=params(2),
        cost_estimate=cost(40_000_000_000, 64 << 20),
        name="signed_units",
    )(in_hbm(gate), in_hbm(up), in_hbm(signs))


def hadamard_128():
    both = lax.broadcasted_iota(jnp.int32, (lanes, lanes), 0) & lax.broadcasted_iota(
        jnp.int32, (lanes, lanes), 1
    )
    for shift in (4, 2, 1):
        both = both ^ (both >> shift)
    return (1 - 2 * (both & 1)).astype(f32).astype(bf16)


def mix_kernel(own_ref, other_ref, wide_ref, send_ref):
    rows, width = own_ref.shape
    matrix = hadamard_128()
    upper = bit_of("hid", 1) == 1
    own, other = own_ref[...].astype(f32), other_ref[...].astype(f32)
    stacked = jnp.concatenate([other, own], axis=0).astype(bf16)
    count = width // lanes
    tall = jnp.concatenate([stacked[:, j * lanes : (j + 1) * lanes] for j in range(count)], axis=0)
    product = jnp.dot(tall, matrix, preferred_element_type=f32)
    blocks = []
    for j in range(count):
        theirs = product[2 * j * rows : (2 * j + 1) * rows]
        mine = product[(2 * j + 1) * rows : (2 * j + 2) * rows]
        blocks.append(theirs + jnp.where(upper, -mine, mine))
    step = 1
    while step < len(blocks):
        for j in range(len(blocks)):
            if not j & step:
                a, b = blocks[j], blocks[j | step]
                blocks[j], blocks[j | step] = a + b, a - b
        step *= 2
    for j, block in enumerate(blocks):
        wide_ref[:, j * lanes : (j + 1) * lanes] = block
        send_ref[:, j * lanes : (j + 1) * lanes] = block.astype(bf16)


def mix(own, other):
    return pl.pallas_call(
        mix_kernel,
        out_shape=(jax.ShapeDtypeStruct(own.shape, f32), jax.ShapeDtypeStruct(own.shape, bf16)),
        in_specs=[VMEM] * 2,
        out_specs=(VMEM, VMEM),
        compiler_params=params(2),
        name="mix",
    )(own, other)


def combine(wide, other, distance, factor):
    def kernel(wide_ref, other_ref, *out_refs):
        own, theirs = wide_ref[...], other_ref[...].astype(f32)
        mixed = theirs + jnp.where(bit_of("hid", distance) == 1, -own, own)
        if factor is None:
            out_refs[0][...] = mixed
            out_refs[1][...] = mixed.astype(bf16)
        else:
            out_refs[0][...] = (mixed * factor).astype(bf16)

    types = (f32, bf16) if factor is None else (bf16,)
    return pl.pallas_call(
        kernel,
        out_shape=tuple(jax.ShapeDtypeStruct(wide.shape, t) for t in types),
        in_specs=[VMEM] * 2,
        out_specs=(VMEM,) * len(types),
        compiler_params=params(2),
        name="combine",
    )(wide, other)


def add(total, arrived, last, first):
    def kernel(total_ref, arrived_ref, *out_refs):
        value = total_ref[...] + arrived_ref[...].astype(f32)
        if not last:
            out_refs[0][...] = value
        out_refs[-1][...] = value.astype(bf16)

    types = (bf16,) if last else (f32, bf16)
    return pl.pallas_call(
        kernel,
        out_shape=tuple(jax.ShapeDtypeStruct(total.shape, t) for t in types),
        in_specs=[VMEM] * 2,
        out_specs=(VMEM,) * len(types),
        compiler_params=params(2, total.shape[0]),
        cost_estimate=cost(40_000_000_000, 0) if not last else None,
        name="add",
    )(total, arrived)


def places(res_rows, own_rows):
    first, me_row = lax.axis_index("hid") * res_rows, lax.axis_index("row")
    found = []
    for r in range(res_rows):
        row = first + r
        found.append(((row // own_rows) ^ me_row) * own_rows + row % own_rows)
    return found


def gather_rows(rows):
    own_rows, depth = rows[0].shape

    def kernel(*refs):
        parts = [ref[...].astype(f32) for ref in refs[:-1]]
        refs[-1][...] = jnp.concatenate(parts, axis=0).astype(bf16)

    return pl.pallas_call(
        kernel,
        out_shape=jax.ShapeDtypeStruct((own_rows * len(rows), depth), bf16),
        in_specs=[VMEM] * len(rows),
        out_specs=VMEM,
        compiler_params=params(2, own_rows * len(rows)),
        name="gather_rows",
    )(*rows)


def down_half(rows, weight, scale, residual, own_rows, other_half, out_type):
    count, depth = rows.shape
    half = weight.shape[1] // 2
    bn = tile_of(half)

    def kernel(x_ref, w_ref, s_ref, r_ref, o_ref):
        side = bit_of("hid", 1)
        if other_half:
            side = 1 - side
        where = places(r_ref.shape[0], own_rows)
        index = lax.broadcasted_iota(jnp.int32, (count, bn), 0)

        for n in range(half // bn):
            there = pl.ds(pl.multiple_of(side * half + n * bn, lanes), bn)
            total = jnp.dot(x_ref[...], w_ref[:, there], preferred_element_type=f32)
            total = total * (s_ref[:, there].astype(f32) * 2.0 ** (-23))
            residual_rows = r_ref[:, there].astype(f32)
            for r, place in enumerate(where):
                total = total + jnp.where(index == place, residual_rows[r : r + 1], 0.0)
            o_ref[:, n * bn : (n + 1) * bn] = total.astype(out_type)

    return pl.pallas_call(
        kernel,
        out_shape=jax.ShapeDtypeStruct((count, half), out_type),
        in_specs=[VMEM] * 4,
        out_specs=VMEM,
        compiler_params=params(14, count),
        cost_estimate=cost(2 * count * depth * half, 2 * depth * half),
        name="down_other" if other_half else "down_own",
    )(rows, weight, scale, residual)


def qkv_half(stream, gain, weight, before, own_rows):
    count, depth = stream.shape
    width = weight.shape[1]
    bn = tile_of(width)
    own_half = before is None
    first_rows = [(0, count)] if own_half else [(0, own_rows), (own_rows, count - own_rows)]

    def kernel(x_ref, g_ref, w_ref, *refs):
        before_ref = None if own_half else refs[0]
        out_refs, scaled = refs[-1 - len(first_rows) : -1], refs[-1]
        side = bit_of("hid", 1)
        if not own_half:
            side = 1 - side
        there = pl.ds(pl.multiple_of(side * depth, depth), depth)
        wide = x_ref[...].astype(f32)
        scaled[...] = (wide * g_ref[:, there].astype(f32)).astype(bf16)
        squares = jnp.broadcast_to(jnp.sum(wide * wide, axis=1, keepdims=True), (count, lanes))

        def put(columns, value):
            if not own_half:
                value = value + before_ref[:, columns]
            for ref, (start, size) in zip(out_refs, first_rows):
                ref[:, columns] = value[start : start + size]

        put(pl.ds(width, lanes), squares)

        for n in range(width // bn):
            columns = pl.ds(n * bn, bn)
            put(columns, jnp.dot(scaled[...], w_ref[there, columns], preferred_element_type=f32))

    operands = (stream, gain, weight) + (() if own_half else (before,))
    return pl.pallas_call(
        kernel,
        out_shape=tuple(jax.ShapeDtypeStruct((size, width + lanes), f32) for _, size in first_rows),
        in_specs=[VMEM] * len(operands),
        out_specs=(VMEM,) * len(first_rows),
        scratch_shapes=[pltpu.VMEM((count, depth), bf16)],
        compiler_params=params(2, count),
        cost_estimate=cost(2 * count * depth * width, 2 * depth * width),
        name="qkv_own" if own_half else "qkv_other",
    )(*operands)


def take_rows(stream, stream_other, res_rows, own_rows):
    count, half = stream.shape

    def kernel(own_ref, other_ref, out_ref):
        index = lax.broadcasted_iota(jnp.int32, (count, half), 0)
        side = bit_of("hid", 1)
        for ref, at in ((own_ref, side), (other_ref, 1 - side)):
            wide = ref[...].astype(f32)
            taken = [
                jnp.sum(jnp.where(index == place, wide, 0.0), axis=0, keepdims=True)
                for place in places(res_rows, own_rows)
            ]
            there = pl.ds(pl.multiple_of(at * half, half), half)
            out_ref[:, there] = jnp.concatenate(taken, axis=0).astype(bf16)

    return pl.pallas_call(
        kernel,
        out_shape=jax.ShapeDtypeStruct((res_rows, 2 * half), bf16),
        in_specs=[VMEM] * 2,
        out_specs=VMEM,
        compiler_params=params(2, count),
        name="take_rows",
    )(stream, stream_other)


def body(
    gate_proj,
    up_proj,
    hadamard_signs,
    down_codes,
    down_scales,
    residual,
    norm_gain,
    qkv_codes,
    qkv_scales,
):
    hid, n_row = lax.axis_size("hid"), lax.axis_size("row")
    own_rows, depth = gate_proj.shape
    res_rows, features = residual.shape
    distances = [1 << b for b in range(hid.bit_length() - 1)]

    send = signed_units(gate_proj, up_proj, hadamard_signs)
    for k, distance in enumerate(distances):
        other = exchange(send, "hid", distance)
        last = k == len(distances) - 1
        if k == 0:
            wide, send = mix(send, other)
        elif not last:
            wide, send = combine(wide, other, distance, None)
        else:
            (rotated,) = combine(wide, other, distance, 1.0 / math.sqrt(depth * hid))
    rows = [rotated] + [exchange(rotated, "row", j) for j in range(1, n_row)]
    rows = gather_rows(rows)

    scale = down_scales.reshape(1, -1)
    theirs = down_half(rows, down_codes, scale, residual, own_rows, True, bf16)
    arrived = exchange(theirs, "hid", 1)
    total = down_half(rows, down_codes, scale, residual, own_rows, False, f32)
    for distance in distances[1:]:
        total, send = add(total, arrived, False, distance == 2)
        arrived = exchange(send, "hid", distance)
    (stream,) = add(total, arrived, True, False)
    stream_other = exchange(stream, "hid", 1)

    gain = norm_gain.reshape(1, -1)
    (part,) = qkv_half(stream, gain, qkv_codes, None, own_rows)
    mine, rest = qkv_half(stream_other, gain, qkv_codes, part, own_rows)
    for j in range(1, n_row):
        mine = mine + exchange(rest[(j - 1) * own_rows : j * own_rows], "row", j)
    width = qkv_codes.shape[1]
    inverse = lax.rsqrt(mine[:, width : width + 1] / (features * n_row) + epsilon)
    joined_qkv = (mine[:, :width] * inverse * (qkv_scales.astype(f32) * 2.0 ** (-22))[None, :]).astype(bf16)
    return (take_rows(stream, stream_other, res_rows, own_rows), joined_qkv)


def solution(mesh):
    return jax.shard_map(
        body,
        mesh=mesh,
        in_specs=(
            P(("groups", "row"), "hid"),
            P(("groups", "row"), "hid"),
            P("hid"),
            P("hid", "row"),
            P("row"),
            P(("groups", "hid"), "row"),
            P("row"),
            P("row", "hid"),
            P("hid"),
        ),
        out_specs=(P(("groups", "hid"), "row"), P(("groups", "row"), "hid")),
        check_vma=False,
    )
```

```python
import math

import jax
import jax.numpy as jnp
from jax import lax
from jax.experimental import pallas as pl
from jax.experimental.pallas import tpu as pltpu
from jax.sharding import PartitionSpec as P

epsilon = 1e-05
lanes = 128
VMEM = pl.BlockSpec(memory_space=pltpu.VMEM)
HBM = pl.BlockSpec(memory_space=pltpu.HBM)
f32, bf16 = jnp.float32, jnp.bfloat16


def exchange(block, axis, distance):
    count = lax.axis_size(axis)
    return lax.ppermute(block, axis, [(i, i ^ distance) for i in range(count)])


def bit_of(axis, distance):
    return lax.axis_index(axis) // distance % 2


def in_hbm(array):
    return pltpu.with_memory_space_constraint(array, pltpu.HBM)


def in_vmem(array):
    return pltpu.with_memory_space_constraint(array, pltpu.VMEM)


def params(mib, rows=16):
    return pltpu.CompilerParams(vmem_limit_bytes=mib * max(1, rows // 16) << 20)


def cost(flops, nbytes):
    return pl.CostEstimate(flops=flops, bytes_accessed=nbytes, transcendentals=0)


def tile_of(width):
    parts = next(p for p in (1, 2, 3, 4, 6, 8, 9, 12) if width // p <= 1152 and width % (p * lanes) == 0)
    return width // parts


def signed_kernel(gate_hbm, up_hbm, sign_hbm, out_ref, gate_ref, up_ref, sign_ref, sems):
    copies = [
        pltpu.make_async_copy(gate_hbm, gate_ref, sems.at[0]),
        pltpu.make_async_copy(up_hbm, up_ref, sems.at[1]),
        pltpu.make_async_copy(sign_hbm, sign_ref, sems.at[2]),
    ]
    for copy in copies:
        copy.start()
    for copy in copies:
        copy.wait()
    gate = gate_ref[...].astype(f32)
    hidden = (gate / (1.0 + jnp.exp(-gate)) * up_ref[...].astype(f32)).astype(bf16)
    flips = (1 - 2 * sign_ref[...]).astype(f32)
    out_ref[...] = (hidden.astype(f32) * flips).astype(bf16)


def signed_units(gate, up, signs):
    signs = signs.reshape(1, -1)
    return pl.pallas_call(
        signed_kernel,
        out_shape=jax.ShapeDtypeStruct(gate.shape, bf16),
        in_specs=[HBM] * 3,
        out_specs=VMEM,
        scratch_shapes=[
            pltpu.VMEM(gate.shape, bf16),
            pltpu.VMEM(gate.shape, bf16),
            pltpu.VMEM(signs.shape, jnp.int32),
            pltpu.SemaphoreType.DMA((3,)),
        ],
        compiler_params=params(2),
        name="signed_units",
    )(in_hbm(gate), in_hbm(up), in_hbm(signs))


def hadamard_128():
    both = lax.broadcasted_iota(jnp.int32, (lanes, lanes), 0) & lax.broadcasted_iota(
        jnp.int32, (lanes, lanes), 1
    )
    for shift in (4, 2, 1):
        both = both ^ (both >> shift)
    return (1 - 2 * (both & 1)).astype(f32).astype(bf16)


def mix_kernel(own_ref, other_ref, wide_ref, send_ref):
    rows, width = own_ref.shape
    matrix = hadamard_128()
    upper = bit_of("hid", 1) == 1
    own, other = own_ref[...].astype(f32), other_ref[...].astype(f32)
    stacked = jnp.concatenate([other, own], axis=0).astype(bf16)
    count = width // lanes
    tall = jnp.concatenate([stacked[:, j * lanes : (j + 1) * lanes] for j in range(count)], axis=0)
    product = jnp.dot(tall, matrix, preferred_element_type=f32)
    blocks = []
    for j in range(count):
        theirs = product[2 * j * rows : (2 * j + 1) * rows]
        mine = product[(2 * j + 1) * rows : (2 * j + 2) * rows]
        blocks.append(theirs + jnp.where(upper, -mine, mine))
    step = 1
    while step < len(blocks):
        for j in range(len(blocks)):
            if not j & step:
                a, b = blocks[j], blocks[j | step]
                blocks[j], blocks[j | step] = a + b, a - b
        step *= 2
    for j, block in enumerate(blocks):
        wide_ref[:, j * lanes : (j + 1) * lanes] = block
        send_ref[:, j * lanes : (j + 1) * lanes] = block.astype(bf16)


def mix(own, other):
    return pl.pallas_call(
        mix_kernel,
        out_shape=(jax.ShapeDtypeStruct(own.shape, f32), jax.ShapeDtypeStruct(own.shape, bf16)),
        in_specs=[VMEM] * 2,
        out_specs=(VMEM, VMEM),
        compiler_params=params(2),
        cost_estimate=cost(400_000_000_000, 0),
        name="mix",
    )(own, other)


def combine(wide, other, distance, factor):
    def kernel(wide_ref, other_ref, *out_refs):
        own, theirs = wide_ref[...], other_ref[...].astype(f32)
        mixed = theirs + jnp.where(bit_of("hid", distance) == 1, -own, own)
        if factor is None:
            out_refs[0][...] = mixed
            out_refs[1][...] = mixed.astype(bf16)
        else:
            out_refs[0][...] = (mixed * factor).astype(bf16)

    types = (f32, bf16) if factor is None else (bf16,)
    return pl.pallas_call(
        kernel,
        out_shape=tuple(jax.ShapeDtypeStruct(wide.shape, t) for t in types),
        in_specs=[VMEM] * 2,
        out_specs=(VMEM,) * len(types),
        compiler_params=params(2),
        name="combine",
    )(wide, other)


def add(total, arrived, last, first):
    def kernel(total_ref, arrived_ref, *out_refs):
        value = total_ref[...] + arrived_ref[...].astype(f32)
        if not last:
            out_refs[0][...] = value
        out_refs[-1][...] = value.astype(bf16)

    types = (bf16,) if last else (f32, bf16)
    return pl.pallas_call(
        kernel,
        out_shape=tuple(jax.ShapeDtypeStruct(total.shape, t) for t in types),
        in_specs=[VMEM] * 2,
        out_specs=(VMEM,) * len(types),
        compiler_params=params(2, total.shape[0]),
        cost_estimate=cost(40_000_000_000, 0) if not last else None,
        name="add",
    )(total, arrived)


def places(res_rows, own_rows):
    first, me_row = lax.axis_index("hid") * res_rows, lax.axis_index("row")
    found = []
    for r in range(res_rows):
        row = first + r
        found.append(((row // own_rows) ^ me_row) * own_rows + row % own_rows)
    return found


def gather_rows(rows):
    own_rows, depth = rows[0].shape

    def kernel(*refs):
        parts = [ref[...].astype(f32) for ref in refs[:-1]]
        refs[-1][...] = jnp.concatenate(parts, axis=0).astype(bf16)

    return pl.pallas_call(
        kernel,
        out_shape=jax.ShapeDtypeStruct((own_rows * len(rows), depth), bf16),
        in_specs=[VMEM] * len(rows),
        out_specs=VMEM,
        compiler_params=params(2, own_rows * len(rows)),
        name="gather_rows",
    )(*rows)


def down_half(rows, weight, scale, residual, own_rows, other_half, out_type):
    count, depth = rows.shape
    half = weight.shape[1] // 2
    bn = tile_of(half)

    def kernel(x_ref, w_ref, s_ref, r_ref, o_ref):
        side = bit_of("hid", 1)
        if other_half:
            side = 1 - side
        where = places(r_ref.shape[0], own_rows)
        index = lax.broadcasted_iota(jnp.int32, (count, bn), 0)

        for n in range(half // bn):
            there = pl.ds(pl.multiple_of(side * half + n * bn, lanes), bn)
            total = jnp.dot(x_ref[...], w_ref[:, there], preferred_element_type=f32)
            total = total * (s_ref[:, there].astype(f32) * 2.0 ** (-23))
            residual_rows = r_ref[:, there].astype(f32)
            for r, place in enumerate(where):
                total = total + jnp.where(index == place, residual_rows[r : r + 1], 0.0)
            o_ref[:, n * bn : (n + 1) * bn] = total.astype(out_type)

    return pl.pallas_call(
        kernel,
        out_shape=jax.ShapeDtypeStruct((count, half), out_type),
        in_specs=[VMEM] * 4,
        out_specs=VMEM,
        compiler_params=params(14, count),
        cost_estimate=cost(2 * count * depth * half, 2 * depth * half),
        name="down_other" if other_half else "down_own",
    )(rows, weight, scale, residual)


def qkv_half(stream, gain, weight, before, own_rows):
    count, depth = stream.shape
    width = weight.shape[1]
    bn = tile_of(width)
    own_half = before is None
    first_rows = [(0, count)] if own_half else [(0, own_rows), (own_rows, count - own_rows)]

    def kernel(x_ref, g_ref, w_ref, *refs):
        before_ref = None if own_half else refs[0]
        out_refs, scaled = refs[-1 - len(first_rows) : -1], refs[-1]
        side = bit_of("hid", 1)
        if not own_half:
            side = 1 - side
        there = pl.ds(pl.multiple_of(side * depth, depth), depth)
        wide = x_ref[...].astype(f32)
        scaled[...] = (wide * g_ref[:, there].astype(f32)).astype(bf16)
        squares = jnp.broadcast_to(jnp.sum(wide * wide, axis=1, keepdims=True), (count, lanes))

        def put(columns, value):
            if not own_half:
                value = value + before_ref[:, columns]
            for ref, (start, size) in zip(out_refs, first_rows):
                ref[:, columns] = value[start : start + size]

        put(pl.ds(width, lanes), squares)

        for n in range(width // bn):
            columns = pl.ds(n * bn, bn)
            put(columns, jnp.dot(scaled[...], w_ref[there, columns], preferred_element_type=f32))

    operands = (stream, gain, weight) + (() if own_half else (before,))
    return pl.pallas_call(
        kernel,
        out_shape=tuple(jax.ShapeDtypeStruct((size, width + lanes), f32) for _, size in first_rows),
        in_specs=[VMEM] * len(operands),
        out_specs=(VMEM,) * len(first_rows),
        scratch_shapes=[pltpu.VMEM((count, depth), bf16)],
        compiler_params=params(2, count),
        cost_estimate=cost(2 * count * depth * width, 2 * depth * width),
        name="qkv_own" if own_half else "qkv_other",
    )(*operands)


def take_rows(stream, stream_other, res_rows, own_rows):
    count, half = stream.shape

    def kernel(own_ref, other_ref, out_ref):
        index = lax.broadcasted_iota(jnp.int32, (count, half), 0)
        side = bit_of("hid", 1)
        for ref, at in ((own_ref, side), (other_ref, 1 - side)):
            wide = ref[...].astype(f32)
            taken = [
                jnp.sum(jnp.where(index == place, wide, 0.0), axis=0, keepdims=True)
                for place in places(res_rows, own_rows)
            ]
            there = pl.ds(pl.multiple_of(at * half, half), half)
            out_ref[:, there] = jnp.concatenate(taken, axis=0).astype(bf16)

    return pl.pallas_call(
        kernel,
        out_shape=jax.ShapeDtypeStruct((res_rows, 2 * half), bf16),
        in_specs=[VMEM] * 2,
        out_specs=VMEM,
        compiler_params=params(2, count),
        name="take_rows",
    )(stream, stream_other)


def finish(mine, arrived, scales, features):
    rows, wide = mine.shape
    width = wide - lanes

    def kernel(*refs):
        mine_ref, scale_ref, out_ref = refs[0], refs[-2], refs[-1]
        total = mine_ref[...]
        for ref in refs[1:-2]:
            total = total + ref[...]
        inverse = lax.rsqrt(total[:, width : width + 1] / features + epsilon)
        output_scale = scale_ref[...].astype(f32) * 2.0 ** (-22)
        out_ref[...] = (total[:, :width] * inverse * output_scale).astype(bf16)

    return pl.pallas_call(
        kernel,
        out_shape=jax.ShapeDtypeStruct((rows, width), bf16),
        in_specs=[VMEM] * (2 + len(arrived)),
        out_specs=VMEM,
        compiler_params=params(2 * (1 + len(arrived))),
        name="finish",
    )(mine, *arrived, scales)


def body(
    gate_proj,
    up_proj,
    hadamard_signs,
    down_codes,
    down_scales,
    residual,
    norm_gain,
    qkv_codes,
    qkv_scales,
):
    hid, n_row = lax.axis_size("hid"), lax.axis_size("row")
    own_rows, depth = gate_proj.shape
    res_rows, features = residual.shape
    distances = [1 << b for b in range(hid.bit_length() - 1)]

    send = signed_units(gate_proj, up_proj, hadamard_signs)
    for k, distance in enumerate(distances):
        other = exchange(send, "hid", distance)
        last = k == len(distances) - 1
        if k == 0:
            wide, send = mix(send, other)
        elif not last:
            wide, send = combine(wide, other, distance, None)
        else:
            (rotated,) = combine(wide, other, distance, 1.0 / math.sqrt(depth * hid))
    rows = [rotated] + [exchange(rotated, "row", j) for j in range(1, n_row)]
    rows = gather_rows(rows)

    scale = down_scales.reshape(1, -1)
    theirs = down_half(rows, down_codes, scale, residual, own_rows, True, bf16)
    arrived = exchange(theirs, "hid", 1)
    total = down_half(rows, down_codes, scale, residual, own_rows, False, f32)
    for distance in distances[1:]:
        total, send = add(total, arrived, False, distance == 2)
        arrived = exchange(send, "hid", distance)
    (stream,) = add(total, arrived, True, False)
    stream_other = exchange(stream, "hid", 1)

    gain = norm_gain.reshape(1, -1)
    (part,) = qkv_half(stream, gain, qkv_codes, None, own_rows)
    mine, rest = qkv_half(stream_other, gain, qkv_codes, part, own_rows)
    arrived = [exchange(rest[(j - 1) * own_rows : j * own_rows], "row", j) for j in range(1, n_row)]
    joined_qkv = finish(mine, arrived, qkv_scales.reshape(1, -1), features * n_row)
    return (take_rows(stream, stream_other, res_rows, own_rows), joined_qkv)


def solution(mesh):
    return jax.shard_map(
        body,
        mesh=mesh,
        in_specs=(
            P(("groups", "row"), "hid"),
            P(("groups", "row"), "hid"),
            P("hid"),
            P("hid", "row"),
            P("row"),
            P(("groups", "hid"), "row"),
            P("row"),
            P("row", "hid"),
            P("hid"),
        ),
        out_specs=(P(("groups", "hid"), "row"), P(("groups", "row"), "hid")),
        check_vma=False,
    )
```

```python
import math

import jax
import jax.numpy as jnp
from jax import lax
from jax.experimental import pallas as pl
from jax.experimental.pallas import tpu as pltpu
from jax.sharding import PartitionSpec as P

epsilon = 1e-05
lanes = 128
VMEM = pl.BlockSpec(memory_space=pltpu.VMEM)
HBM = pl.BlockSpec(memory_space=pltpu.HBM)
f32, bf16 = jnp.float32, jnp.bfloat16


def exchange(block, axis, distance):
    count = lax.axis_size(axis)
    return lax.ppermute(block, axis, [(i, i ^ distance) for i in range(count)])


def bit_of(axis, distance):
    return lax.axis_index(axis) // distance % 2


def in_hbm(array):
    return pltpu.with_memory_space_constraint(array, pltpu.HBM)


def in_vmem(array):
    return pltpu.with_memory_space_constraint(array, pltpu.VMEM)


def params(mib, rows=16):
    return pltpu.CompilerParams(vmem_limit_bytes=mib * max(1, rows // 16) << 20)


def cost(flops, nbytes):
    return pl.CostEstimate(flops=flops, bytes_accessed=nbytes, transcendentals=0)


def tile_of(width):
    parts = next(p for p in (1, 2, 3, 4, 6, 8, 9, 12) if width // p <= 1152 and width % (p * lanes) == 0)
    return width // parts


def signed_kernel(gate_hbm, up_hbm, sign_hbm, out_ref, gate_ref, up_ref, sign_ref, sems):
    copies = [
        pltpu.make_async_copy(gate_hbm, gate_ref, sems.at[0]),
        pltpu.make_async_copy(up_hbm, up_ref, sems.at[1]),
        pltpu.make_async_copy(sign_hbm, sign_ref, sems.at[2]),
    ]
    for copy in copies:
        copy.start()
    for copy in copies:
        copy.wait()
    gate = gate_ref[...].astype(f32)
    hidden = (gate / (1.0 + jnp.exp(-gate)) * up_ref[...].astype(f32)).astype(bf16)
    flips = (1 - 2 * sign_ref[...]).astype(f32)
    out_ref[...] = (hidden.astype(f32) * flips).astype(bf16)


def signed_units(gate, up, signs):
    signs = signs.reshape(1, -1)
    return pl.pallas_call(
        signed_kernel,
        out_shape=jax.ShapeDtypeStruct(gate.shape, bf16),
        in_specs=[HBM] * 3,
        out_specs=VMEM,
        scratch_shapes=[
            pltpu.VMEM(gate.shape, bf16),
            pltpu.VMEM(gate.shape, bf16),
            pltpu.VMEM(signs.shape, jnp.int32),
            pltpu.SemaphoreType.DMA((3,)),
        ],
        compiler_params=params(2),
        name="signed_units",
    )(in_hbm(gate), in_hbm(up), in_hbm(signs))


def hadamard_128():
    both = lax.broadcasted_iota(jnp.int32, (lanes, lanes), 0) & lax.broadcasted_iota(
        jnp.int32, (lanes, lanes), 1
    )
    for shift in (4, 2, 1):
        both = both ^ (both >> shift)
    return (1 - 2 * (both & 1)).astype(f32).astype(bf16)


def mix_kernel(own_ref, other_ref, wide_ref, send_ref):
    rows, width = own_ref.shape
    matrix = hadamard_128()
    upper = bit_of("hid", 1) == 1
    own, other = own_ref[...].astype(f32), other_ref[...].astype(f32)
    stacked = jnp.concatenate([other, own], axis=0).astype(bf16)
    count = width // lanes
    tall = jnp.concatenate([stacked[:, j * lanes : (j + 1) * lanes] for j in range(count)], axis=0)
    product = jnp.dot(tall, matrix, preferred_element_type=f32)
    blocks = []
    for j in range(count):
        theirs = product[2 * j * rows : (2 * j + 1) * rows]
        mine = product[(2 * j + 1) * rows : (2 * j + 2) * rows]
        blocks.append(theirs + jnp.where(upper, -mine, mine))
    step = 1
    while step < len(blocks):
        for j in range(len(blocks)):
            if not j & step:
                a, b = blocks[j], blocks[j | step]
                blocks[j], blocks[j | step] = a + b, a - b
        step *= 2
    for j, block in enumerate(blocks):
        wide_ref[:, j * lanes : (j + 1) * lanes] = block
        send_ref[:, j * lanes : (j + 1) * lanes] = block.astype(bf16)


def mix(own, other):
    return pl.pallas_call(
        mix_kernel,
        out_shape=(jax.ShapeDtypeStruct(own.shape, f32), jax.ShapeDtypeStruct(own.shape, bf16)),
        in_specs=[VMEM] * 2,
        out_specs=(VMEM, VMEM),
        compiler_params=params(2),
        cost_estimate=cost(400_000_000_000, 0),
        name="mix",
    )(own, other)


def combine(wide, others, masks, bits, factor):
    def kernel(*refs):
        out_refs = refs[1 + len(others) :]
        mixed = None
        for ref, mask in zip(refs, [0] + masks):
            value = ref[...].astype(f32)
            flips = [bit_of("hid", 1 << bit) for bit in bits if not mask >> bit & 1]
            if flips:
                value = jnp.where(sum(flips) % 2 == 1, -value, value)
            mixed = value if mixed is None else mixed + value
        if factor is None:
            out_refs[0][...] = mixed
            out_refs[1][...] = mixed.astype(bf16)
        else:
            out_refs[0][...] = (mixed * factor).astype(bf16)

    types = (f32, bf16) if factor is None else (bf16,)
    return pl.pallas_call(
        kernel,
        out_shape=tuple(jax.ShapeDtypeStruct(wide.shape, t) for t in types),
        in_specs=[VMEM] * (1 + len(others)),
        out_specs=(VMEM,) * len(types),
        compiler_params=params(2),
        name="combine",
    )(wide, *others)


def add(total, arrived, last, estimate):
    def kernel(*refs):
        out_refs = refs[1 + len(arrived) :]
        value = refs[0][...]
        for ref in refs[1 : 1 + len(arrived)]:
            value = value + ref[...].astype(f32)
        if not last:
            out_refs[0][...] = value
        out_refs[-1][...] = value.astype(bf16)

    types = (bf16,) if last else (f32, bf16)
    return pl.pallas_call(
        kernel,
        out_shape=tuple(jax.ShapeDtypeStruct(total.shape, t) for t in types),
        in_specs=[VMEM] * (1 + len(arrived)),
        out_specs=(VMEM,) * len(types),
        compiler_params=params(2, total.shape[0]),
        cost_estimate=estimate,
        name="add",
    )(total, *arrived)


def places(res_rows, own_rows):
    first, me_row = lax.axis_index("hid") * res_rows, lax.axis_index("row")
    found = []
    for r in range(res_rows):
        row = first + r
        found.append(((row // own_rows) ^ me_row) * own_rows + row % own_rows)
    return found


def gather_rows(rows):
    own_rows, depth = rows[0].shape

    def kernel(*refs):
        parts = [ref[...].astype(f32) for ref in refs[:-1]]
        refs[-1][...] = jnp.concatenate(parts, axis=0).astype(bf16)

    return pl.pallas_call(
        kernel,
        out_shape=jax.ShapeDtypeStruct((own_rows * len(rows), depth), bf16),
        in_specs=[VMEM] * len(rows),
        out_specs=VMEM,
        compiler_params=params(2, own_rows * len(rows)),
        name="gather_rows",
    )(*rows)


def down_half(rows, weight, scale, residual, own_rows, other_half, out_type):
    count, depth = rows.shape
    half = weight.shape[1] // 2
    bn = tile_of(half)

    def kernel(x_ref, w_ref, s_ref, r_ref, o_ref):
        side = bit_of("hid", 1)
        if other_half:
            side = 1 - side
        where = places(r_ref.shape[0], own_rows)
        index = lax.broadcasted_iota(jnp.int32, (count, bn), 0)

        for n in range(half // bn):
            there = pl.ds(pl.multiple_of(side * half + n * bn, lanes), bn)
            total = jnp.dot(x_ref[...], w_ref[:, there], preferred_element_type=f32)
            total = total * (s_ref[:, there].astype(f32) * 2.0 ** (-23))
            residual_rows = r_ref[:, there].astype(f32)
            for r, place in enumerate(where):
                total = total + jnp.where(index == place, residual_rows[r : r + 1], 0.0)
            o_ref[:, n * bn : (n + 1) * bn] = total.astype(out_type)

    return pl.pallas_call(
        kernel,
        out_shape=jax.ShapeDtypeStruct((count, half), out_type),
        in_specs=[VMEM] * 4,
        out_specs=VMEM,
        compiler_params=params(14, count),
        cost_estimate=cost(2 * count * depth * half, 2 * depth * half),
        name="down_other" if other_half else "down_own",
    )(rows, weight, scale, residual)


def qkv_half(stream, gain, weight, before, own_rows):
    count, depth = stream.shape
    width = weight.shape[1]
    bn = tile_of(width)
    own_half = before is None
    first_rows = [(0, count)] if own_half else [(0, own_rows), (own_rows, count - own_rows)]

    def kernel(x_ref, g_ref, w_ref, *refs):
        before_ref = None if own_half else refs[0]
        out_refs, scaled = refs[-1 - len(first_rows) : -1], refs[-1]
        side = bit_of("hid", 1)
        if not own_half:
            side = 1 - side
        there = pl.ds(pl.multiple_of(side * depth, depth), depth)
        wide = x_ref[...].astype(f32)
        scaled[...] = (wide * g_ref[:, there].astype(f32)).astype(bf16)
        squares = jnp.broadcast_to(jnp.sum(wide * wide, axis=1, keepdims=True), (count, lanes))

        def put(columns, value):
            if not own_half:
                value = value + before_ref[:, columns]
            for ref, (start, size) in zip(out_refs, first_rows):
                ref[:, columns] = value[start : start + size]

        put(pl.ds(width, lanes), squares)

        for n in range(width // bn):
            columns = pl.ds(n * bn, bn)
            put(columns, jnp.dot(scaled[...], w_ref[there, columns], preferred_element_type=f32))

    operands = (stream, gain, weight) + (() if own_half else (before,))
    return pl.pallas_call(
        kernel,
        out_shape=tuple(jax.ShapeDtypeStruct((size, width + lanes), f32) for _, size in first_rows),
        in_specs=[VMEM] * len(operands),
        out_specs=(VMEM,) * len(first_rows),
        scratch_shapes=[pltpu.VMEM((count, depth), bf16)],
        compiler_params=params(2, count),
        cost_estimate=cost(2 * count * depth * width, 2 * depth * width),
        name="qkv_own" if own_half else "qkv_other",
    )(*operands)


def take_rows(stream, stream_other, res_rows, own_rows):
    count, half = stream.shape

    def kernel(own_ref, other_ref, out_ref):
        index = lax.broadcasted_iota(jnp.int32, (count, half), 0)
        side = bit_of("hid", 1)
        for ref, at in ((own_ref, side), (other_ref, 1 - side)):
            wide = ref[...].astype(f32)
            taken = [
                jnp.sum(jnp.where(index == place, wide, 0.0), axis=0, keepdims=True)
                for place in places(res_rows, own_rows)
            ]
            there = pl.ds(pl.multiple_of(at * half, half), half)
            out_ref[:, there] = jnp.concatenate(taken, axis=0).astype(bf16)

    return pl.pallas_call(
        kernel,
        out_shape=jax.ShapeDtypeStruct((res_rows, 2 * half), bf16),
        in_specs=[VMEM] * 2,
        out_specs=VMEM,
        compiler_params=params(2, count),
        name="take_rows",
    )(stream, stream_other)


def finish(mine, arrived, scales, features):
    rows, wide = mine.shape
    width = wide - lanes

    def kernel(*refs):
        mine_ref, scale_ref, out_ref = refs[0], refs[-2], refs[-1]
        total = mine_ref[...]
        for ref in refs[1:-2]:
            total = total + ref[...]
        inverse = lax.rsqrt(total[:, width : width + 1] / features + epsilon)
        output_scale = scale_ref[...].astype(f32) * 2.0 ** (-22)
        out_ref[...] = (total[:, :width] * inverse * output_scale).astype(bf16)

    return pl.pallas_call(
        kernel,
        out_shape=jax.ShapeDtypeStruct((rows, width), bf16),
        in_specs=[VMEM] * (2 + len(arrived)),
        out_specs=VMEM,
        compiler_params=params(2 * (1 + len(arrived))),
        name="finish",
    )(mine, *arrived, scales)


def body(
    gate_proj,
    up_proj,
    hadamard_signs,
    down_codes,
    down_scales,
    residual,
    norm_gain,
    qkv_codes,
    qkv_scales,
):
    hid, n_row = lax.axis_size("hid"), lax.axis_size("row")
    own_rows, depth = gate_proj.shape
    res_rows, features = residual.shape
    count = hid.bit_length() - 1
    steps = [[0]] + [list(range(b, min(b + 2, count))) for b in range(1, count, 2)]
    partners = [[m for m in range(hid - 1, 0, -1) if not m & ~sum(1 << b for b in bits)] for bits in steps]

    send = signed_units(gate_proj, up_proj, hadamard_signs)
    for k, (bits, masks) in enumerate(zip(steps, partners)):
        others = [exchange(send, "hid", mask) for mask in masks]
        if k == 0:
            wide, send = mix(send, *others)
        elif k < len(steps) - 1:
            wide, send = combine(wide, others, masks, bits, None)
        else:
            (rotated,) = combine(wide, others, masks, bits, 1.0 / math.sqrt(depth * hid))
    rows = [rotated] + [exchange(rotated, "row", j) for j in range(1, n_row)]
    rows = gather_rows(rows)

    scale = down_scales.reshape(1, -1)
    theirs = down_half(rows, down_codes, scale, residual, own_rows, True, bf16)
    arrived = exchange(theirs, "hid", 1)
    total = down_half(rows, down_codes, scale, residual, own_rows, False, f32)
    arrived = [arrived]
    for k, masks in enumerate(partners[1:]):
        total, send = add(total, arrived, False, cost(100_000_000_000, 0) if k == 0 else None)
        arrived = [exchange(send, "hid", mask) for mask in masks]
    (stream,) = add(total, arrived, True, None)
    stream_other = exchange(stream, "hid", 1)

    gain = norm_gain.reshape(1, -1)
    (part,) = qkv_half(stream, gain, qkv_codes, None, own_rows)
    mine, rest = qkv_half(stream_other, gain, qkv_codes, part, own_rows)
    arrived = [exchange(rest[(j - 1) * own_rows : j * own_rows], "row", j) for j in range(1, n_row)]
    joined_qkv = finish(mine, arrived, qkv_scales.reshape(1, -1), features * n_row)
    return (take_rows(stream, stream_other, res_rows, own_rows), joined_qkv)


def solution(mesh):
    return jax.shard_map(
        body,
        mesh=mesh,
        in_specs=(
            P(("groups", "row"), "hid"),
            P(("groups", "row"), "hid"),
            P("hid"),
            P("hid", "row"),
            P("row"),
            P(("groups", "hid"), "row"),
            P("row"),
            P("row", "hid"),
            P("hid"),
        ),
        out_specs=(P(("groups", "hid"), "row"), P(("groups", "row"), "hid")),
        check_vma=False,
    )
```

```python
import math

import jax
import jax.numpy as jnp
from jax import lax
from jax.experimental import pallas as pl
from jax.experimental.pallas import tpu as pltpu
from jax.sharding import PartitionSpec as P

epsilon = 1e-05
lanes = 128
VMEM = pl.BlockSpec(memory_space=pltpu.VMEM)
HBM = pl.BlockSpec(memory_space=pltpu.HBM)
f32, bf16 = jnp.float32, jnp.bfloat16


def exchange(block, axis, distance):
    count = lax.axis_size(axis)
    return lax.ppermute(block, axis, [(i, i ^ distance) for i in range(count)])


def bit_of(axis, distance):
    return lax.axis_index(axis) // distance % 2


def in_hbm(array):
    return pltpu.with_memory_space_constraint(array, pltpu.HBM)


def in_vmem(array):
    return pltpu.with_memory_space_constraint(array, pltpu.VMEM)


def params(mib, rows=16):
    return pltpu.CompilerParams(vmem_limit_bytes=mib * max(1, rows // 16) << 20)


def cost(flops, nbytes):
    return pl.CostEstimate(flops=flops, bytes_accessed=nbytes, transcendentals=0)


def tile_of(width):
    parts = next(p for p in (1, 2, 3, 4, 6, 8, 9, 12) if width // p <= 1152 and width % (p * lanes) == 0)
    return width // parts


def signed_kernel(gate_hbm, up_hbm, sign_hbm, out_ref, gate_ref, up_ref, sign_ref, sems):
    copies = [
        pltpu.make_async_copy(gate_hbm, gate_ref, sems.at[0]),
        pltpu.make_async_copy(up_hbm, up_ref, sems.at[1]),
        pltpu.make_async_copy(sign_hbm, sign_ref, sems.at[2]),
    ]
    for copy in copies:
        copy.start()
    for copy in copies:
        copy.wait()
    gate = gate_ref[...].astype(f32)
    hidden = (gate / (1.0 + jnp.exp(-gate)) * up_ref[...].astype(f32)).astype(bf16)
    flips = (1 - 2 * sign_ref[...]).astype(f32)
    out_ref[...] = (hidden.astype(f32) * flips).astype(bf16)


def signed_units(gate, up, signs):
    signs = signs.reshape(1, -1)
    return pl.pallas_call(
        signed_kernel,
        out_shape=jax.ShapeDtypeStruct(gate.shape, bf16),
        in_specs=[HBM] * 3,
        out_specs=VMEM,
        scratch_shapes=[
            pltpu.VMEM(gate.shape, bf16),
            pltpu.VMEM(gate.shape, bf16),
            pltpu.VMEM(signs.shape, jnp.int32),
            pltpu.SemaphoreType.DMA((3,)),
        ],
        compiler_params=params(2),
        cost_estimate=cost(40_000_000_000, 0),
        name="signed_units",
    )(in_hbm(gate), in_hbm(up), in_hbm(signs))


def hadamard_128():
    both = lax.broadcasted_iota(jnp.int32, (lanes, lanes), 0) & lax.broadcasted_iota(
        jnp.int32, (lanes, lanes), 1
    )
    for shift in (4, 2, 1):
        both = both ^ (both >> shift)
    return (1 - 2 * (both & 1)).astype(f32).astype(bf16)


def mix_kernel(own_ref, other_ref, wide_ref, send_ref):
    rows, width = own_ref.shape
    matrix = hadamard_128()
    upper = bit_of("hid", 1) == 1
    own, other = own_ref[...].astype(f32), other_ref[...].astype(f32)
    stacked = jnp.concatenate([other, own], axis=0).astype(bf16)
    count = width // lanes
    tall = jnp.concatenate([stacked[:, j * lanes : (j + 1) * lanes] for j in range(count)], axis=0)
    product = jnp.dot(tall, matrix, preferred_element_type=f32)
    blocks = []
    for j in range(count):
        theirs = product[2 * j * rows : (2 * j + 1) * rows]
        mine = product[(2 * j + 1) * rows : (2 * j + 2) * rows]
        blocks.append(theirs + jnp.where(upper, -mine, mine))
    step = 1
    while step < len(blocks):
        for j in range(len(blocks)):
            if not j & step:
                a, b = blocks[j], blocks[j | step]
                blocks[j], blocks[j | step] = a + b, a - b
        step *= 2
    for j, block in enumerate(blocks):
        wide_ref[:, j * lanes : (j + 1) * lanes] = block
        send_ref[:, j * lanes : (j + 1) * lanes] = block.astype(bf16)


def mix(own, other):
    return pl.pallas_call(
        mix_kernel,
        out_shape=(jax.ShapeDtypeStruct(own.shape, f32), jax.ShapeDtypeStruct(own.shape, bf16)),
        in_specs=[VMEM] * 2,
        out_specs=(VMEM, VMEM),
        compiler_params=params(2),
        name="mix",
    )(own, other)


def combine(wide, others, masks, bits, factor):
    def kernel(*refs):
        out_refs = refs[1 + len(others) :]
        mixed = None
        for ref, mask in zip(refs, [0] + masks):
            value = ref[...].astype(f32)
            flips = [bit_of("hid", 1 << bit) for bit in bits if not mask >> bit & 1]
            if flips:
                value = jnp.where(sum(flips) % 2 == 1, -value, value)
            mixed = value if mixed is None else mixed + value
        if factor is None:
            out_refs[0][...] = mixed
            out_refs[1][...] = mixed.astype(bf16)
        else:
            out_refs[0][...] = (mixed * factor).astype(bf16)

    types = (f32, bf16) if factor is None else (bf16,)
    return pl.pallas_call(
        kernel,
        out_shape=tuple(jax.ShapeDtypeStruct(wide.shape, t) for t in types),
        in_specs=[VMEM] * (1 + len(others)),
        out_specs=(VMEM,) * len(types),
        compiler_params=params(2),
        name="combine",
    )(wide, *others)


def add(total, arrived, last, estimate):
    def kernel(*refs):
        out_refs = refs[1 + len(arrived) :]
        value = refs[0][...]
        for ref in refs[1 : 1 + len(arrived)]:
            value = value + ref[...].astype(f32)
        if not last:
            out_refs[0][...] = value
        out_refs[-1][...] = value.astype(bf16)

    types = (bf16,) if last else (f32, bf16)
    return pl.pallas_call(
        kernel,
        out_shape=tuple(jax.ShapeDtypeStruct(total.shape, t) for t in types),
        in_specs=[VMEM] * (1 + len(arrived)),
        out_specs=(VMEM,) * len(types),
        compiler_params=params(2, total.shape[0]),
        cost_estimate=estimate,
        name="add",
    )(total, *arrived)


def places(res_rows, own_rows):
    first, me_row = lax.axis_index("hid") * res_rows, lax.axis_index("row")
    found = []
    for r in range(res_rows):
        row = first + r
        found.append(((row // own_rows) ^ me_row) * own_rows + row % own_rows)
    return found


def gather_rows(rows):
    own_rows, depth = rows[0].shape

    def kernel(*refs):
        parts = [ref[...].astype(f32) for ref in refs[:-1]]
        refs[-1][...] = jnp.concatenate(parts, axis=0).astype(bf16)

    return pl.pallas_call(
        kernel,
        out_shape=jax.ShapeDtypeStruct((own_rows * len(rows), depth), bf16),
        in_specs=[VMEM] * len(rows),
        out_specs=VMEM,
        compiler_params=params(2, own_rows * len(rows)),
        name="gather_rows",
    )(*rows)


def down_half(rows, weight, scale, residual, own_rows, other_half, out_type):
    count, depth = rows.shape
    half = weight.shape[1] // 2
    bn = tile_of(half)

    def kernel(x_ref, w_ref, s_ref, r_ref, o_ref):
        side = bit_of("hid", 1)
        if other_half:
            side = 1 - side
        where = places(r_ref.shape[0], own_rows)
        index = lax.broadcasted_iota(jnp.int32, (count, bn), 0)

        for n in range(half // bn):
            there = pl.ds(pl.multiple_of(side * half + n * bn, lanes), bn)
            total = jnp.dot(x_ref[...], w_ref[:, there], preferred_element_type=f32)
            total = total * (s_ref[:, there].astype(f32) * 2.0 ** (-23))
            residual_rows = r_ref[:, there].astype(f32)
            for r, place in enumerate(where):
                total = total + jnp.where(index == place, residual_rows[r : r + 1], 0.0)
            o_ref[:, n * bn : (n + 1) * bn] = total.astype(out_type)

    return pl.pallas_call(
        kernel,
        out_shape=jax.ShapeDtypeStruct((count, half), out_type),
        in_specs=[VMEM] * 4,
        out_specs=VMEM,
        compiler_params=params(14, count),
        cost_estimate=cost(2 * count * depth * half, 2 * depth * half),
        name="down_other" if other_half else "down_own",
    )(rows, weight, scale, residual)


def qkv_half(stream, gain, weight, before, own_rows):
    count, depth = stream.shape
    width = weight.shape[1]
    bn = tile_of(width)
    own_half = before is None
    first_rows = [(0, count)] if own_half else [(0, own_rows), (own_rows, count - own_rows)]

    def kernel(x_ref, g_ref, w_ref, *refs):
        before_ref = None if own_half else refs[0]
        out_refs, scaled = refs[-1 - len(first_rows) : -1], refs[-1]
        side = bit_of("hid", 1)
        if not own_half:
            side = 1 - side
        there = pl.ds(pl.multiple_of(side * depth, depth), depth)
        wide = x_ref[...].astype(f32)
        scaled[...] = (wide * g_ref[:, there].astype(f32)).astype(bf16)
        squares = jnp.broadcast_to(jnp.sum(wide * wide, axis=1, keepdims=True), (count, lanes))

        def put(columns, value):
            if not own_half:
                value = value + before_ref[:, columns]
            for ref, (start, size) in zip(out_refs, first_rows):
                ref[:, columns] = value[start : start + size]

        put(pl.ds(width, lanes), squares)

        for n in range(width // bn):
            columns = pl.ds(n * bn, bn)
            put(columns, jnp.dot(scaled[...], w_ref[there, columns], preferred_element_type=f32))

    operands = (stream, gain, weight) + (() if own_half else (before,))
    return pl.pallas_call(
        kernel,
        out_shape=tuple(jax.ShapeDtypeStruct((size, width + lanes), f32) for _, size in first_rows),
        in_specs=[VMEM] * len(operands),
        out_specs=(VMEM,) * len(first_rows),
        scratch_shapes=[pltpu.VMEM((count, depth), bf16)],
        compiler_params=params(2, count),
        cost_estimate=cost(2 * count * depth * width, 2 * depth * width),
        name="qkv_own" if own_half else "qkv_other",
    )(*operands)


def take_rows(stream, stream_other, res_rows, own_rows):
    count, half = stream.shape

    def kernel(own_ref, other_ref, out_ref):
        index = lax.broadcasted_iota(jnp.int32, (count, half), 0)
        side = bit_of("hid", 1)
        for ref, at in ((own_ref, side), (other_ref, 1 - side)):
            wide = ref[...].astype(f32)
            taken = [
                jnp.sum(jnp.where(index == place, wide, 0.0), axis=0, keepdims=True)
                for place in places(res_rows, own_rows)
            ]
            there = pl.ds(pl.multiple_of(at * half, half), half)
            out_ref[:, there] = jnp.concatenate(taken, axis=0).astype(bf16)

    return pl.pallas_call(
        kernel,
        out_shape=jax.ShapeDtypeStruct((res_rows, 2 * half), bf16),
        in_specs=[VMEM] * 2,
        out_specs=VMEM,
        compiler_params=params(2, count),
        name="take_rows",
    )(stream, stream_other)


def finish(mine, arrived, scales, features):
    rows, wide = mine.shape
    width = wide - lanes

    def kernel(*refs):
        mine_ref, scale_ref, out_ref = refs[0], refs[-2], refs[-1]
        total = mine_ref[...]
        for ref in refs[1:-2]:
            total = total + ref[...]
        inverse = lax.rsqrt(total[:, width : width + 1] / features + epsilon)
        output_scale = scale_ref[...].astype(f32) * 2.0 ** (-22)
        out_ref[...] = (total[:, :width] * inverse * output_scale).astype(bf16)

    return pl.pallas_call(
        kernel,
        out_shape=jax.ShapeDtypeStruct((rows, width), bf16),
        in_specs=[VMEM] * (2 + len(arrived)),
        out_specs=VMEM,
        compiler_params=params(2 * (1 + len(arrived))),
        name="finish",
    )(mine, *arrived, scales)


def body(
    gate_proj,
    up_proj,
    hadamard_signs,
    down_codes,
    down_scales,
    residual,
    norm_gain,
    qkv_codes,
    qkv_scales,
):
    hid, n_row = lax.axis_size("hid"), lax.axis_size("row")
    own_rows, depth = gate_proj.shape
    res_rows, features = residual.shape
    count = hid.bit_length() - 1
    steps = [[0]] + [list(range(b, min(b + 2, count))) for b in range(1, count, 2)]
    partners = [[1 << b[0]] if len(b) == 1 else [1 << b[1], 1 << b[0] | 1 << b[1], 1 << b[0]] for b in steps]

    send = signed_units(gate_proj, up_proj, hadamard_signs)
    for k, (bits, masks) in enumerate(zip(steps, partners)):
        others = [exchange(send, "hid", mask) for mask in masks]
        if k == 0:
            wide, send = mix(send, *others)
        elif k < len(steps) - 1:
            wide, send = combine(wide, others, masks, bits, None)
        else:
            (rotated,) = combine(wide, others, masks, bits, 1.0 / math.sqrt(depth * hid))
    rows = [rotated] + [exchange(rotated, "row", j) for j in range(1, n_row)]
    rows = gather_rows(rows)

    scale = down_scales.reshape(1, -1)
    theirs = down_half(rows, down_codes, scale, residual, own_rows, True, bf16)
    arrived = exchange(theirs, "hid", 1)
    total = down_half(rows, down_codes, scale, residual, own_rows, False, f32)
    arrived = [arrived]
    for k, masks in enumerate(partners[1:]):
        total, send = add(total, arrived, False, cost(100_000_000_000, 0) if k == 0 else None)
        arrived = [exchange(send, "hid", mask) for mask in masks]
    (stream,) = add(total, arrived, True, None)
    stream_other = exchange(stream, "hid", 1)

    gain = norm_gain.reshape(1, -1)
    (part,) = qkv_half(stream, gain, qkv_codes, None, own_rows)
    mine, rest = qkv_half(stream_other, gain, qkv_codes, part, own_rows)
    arrived = [exchange(rest[(j - 1) * own_rows : j * own_rows], "row", j) for j in range(1, n_row)]
    joined_qkv = finish(mine, arrived, qkv_scales.reshape(1, -1), features * n_row)
    return (take_rows(stream, stream_other, res_rows, own_rows), joined_qkv)


def solution(mesh):
    return jax.shard_map(
        body,
        mesh=mesh,
        in_specs=(
            P(("groups", "row"), "hid"),
            P(("groups", "row"), "hid"),
            P("hid"),
            P("hid", "row"),
            P("row"),
            P(("groups", "hid"), "row"),
            P("row"),
            P("row", "hid"),
            P("hid"),
        ),
        out_specs=(P(("groups", "hid"), "row"), P(("groups", "row"), "hid")),
        check_vma=False,
    )
```

```python
import math

import jax
import jax.numpy as jnp
from jax import lax
from jax.experimental import pallas as pl
from jax.experimental.pallas import tpu as pltpu
from jax.sharding import PartitionSpec as P

epsilon = 1e-05
lanes = 128
VMEM = pl.BlockSpec(memory_space=pltpu.VMEM)
HBM = pl.BlockSpec(memory_space=pltpu.HBM)
f32, bf16 = jnp.float32, jnp.bfloat16


def exchange(block, axis, distance):
    count = lax.axis_size(axis)
    return lax.ppermute(block, axis, [(i, i ^ distance) for i in range(count)])


def bit_of(axis, distance):
    return lax.axis_index(axis) // distance % 2


def in_hbm(array):
    return pltpu.with_memory_space_constraint(array, pltpu.HBM)


def in_vmem(array):
    return pltpu.with_memory_space_constraint(array, pltpu.VMEM)


def params(mib, rows=16):
    return pltpu.CompilerParams(vmem_limit_bytes=mib * max(1, rows // 16) << 20)


def cost(flops, nbytes):
    return pl.CostEstimate(flops=flops, bytes_accessed=nbytes, transcendentals=0)


def tile_of(width):
    parts = next(p for p in (1, 2, 3, 4, 6, 8, 9, 12) if width // p <= 2304 and width % (p * lanes) == 0)
    return width // parts


def signed_kernel(gate_hbm, up_hbm, sign_hbm, out_ref, gate_ref, up_ref, sign_ref, sems):
    copies = [
        pltpu.make_async_copy(gate_hbm, gate_ref, sems.at[0]),
        pltpu.make_async_copy(up_hbm, up_ref, sems.at[1]),
        pltpu.make_async_copy(sign_hbm, sign_ref, sems.at[2]),
    ]
    for copy in copies:
        copy.start()
    for copy in copies:
        copy.wait()
    gate = gate_ref[...].astype(f32)
    hidden = (gate / (1.0 + jnp.exp(-gate)) * up_ref[...].astype(f32)).astype(bf16)
    flips = (1 - 2 * sign_ref[...]).astype(f32)
    out_ref[...] = (hidden.astype(f32) * flips).astype(bf16)


def signed_units(gate, up, signs):
    signs = signs.reshape(1, -1)
    return pl.pallas_call(
        signed_kernel,
        out_shape=jax.ShapeDtypeStruct(gate.shape, bf16),
        in_specs=[HBM] * 3,
        out_specs=VMEM,
        scratch_shapes=[
            pltpu.VMEM(gate.shape, bf16),
            pltpu.VMEM(gate.shape, bf16),
            pltpu.VMEM(signs.shape, jnp.int32),
            pltpu.SemaphoreType.DMA((3,)),
        ],
        compiler_params=params(2),
        cost_estimate=cost(40_000_000_000, 0),
        name="signed_units",
    )(in_hbm(gate), in_hbm(up), in_hbm(signs))


def hadamard_128():
    both = lax.broadcasted_iota(jnp.int32, (lanes, lanes), 0) & lax.broadcasted_iota(
        jnp.int32, (lanes, lanes), 1
    )
    for shift in (4, 2, 1):
        both = both ^ (both >> shift)
    return (1 - 2 * (both & 1)).astype(f32).astype(bf16)


def lane_blocks(ref, matrix):
    rows, width = ref.shape
    wide = ref[...].astype(f32)
    blocks = [wide[:, j * lanes : (j + 1) * lanes] for j in range(width // lanes)]
    tall = jnp.concatenate(blocks, axis=0).astype(bf16)
    product = jnp.dot(tall, matrix, preferred_element_type=f32)
    return [product[j * rows : (j + 1) * rows] for j in range(len(blocks))]


def own_lanes(own):
    def kernel(own_ref, mixed_ref, matrix_ref):
        matrix = hadamard_128()
        matrix_ref[...] = matrix
        sign = (1 - 2 * bit_of("hid", 1)).astype(f32)
        for j, block in enumerate(lane_blocks(own_ref, matrix)):
            mixed_ref[:, j * lanes : (j + 1) * lanes] = block * sign

    return pl.pallas_call(
        kernel,
        out_shape=(jax.ShapeDtypeStruct(own.shape, f32), jax.ShapeDtypeStruct((lanes, lanes), bf16)),
        in_specs=[VMEM],
        out_specs=(VMEM, VMEM),
        compiler_params=params(2),
        name="own_lanes",
    )(own)


def mix(own, other):
    def kernel(mixed_ref, matrix_ref, other_ref, wide_ref, send_ref):
        blocks = [
            block + mixed_ref[:, j * lanes : (j + 1) * lanes]
            for j, block in enumerate(lane_blocks(other_ref, matrix_ref[...]))
        ]
        step = 1
        while step < len(blocks):
            for j in range(len(blocks)):
                if not j & step:
                    a, b = blocks[j], blocks[j | step]
                    blocks[j], blocks[j | step] = a + b, a - b
            step *= 2
        for j, block in enumerate(blocks):
            wide_ref[:, j * lanes : (j + 1) * lanes] = block
            send_ref[:, j * lanes : (j + 1) * lanes] = block.astype(bf16)

    return pl.pallas_call(
        kernel,
        out_shape=(jax.ShapeDtypeStruct(other.shape, f32), jax.ShapeDtypeStruct(other.shape, bf16)),
        in_specs=[VMEM] * 3,
        out_specs=(VMEM, VMEM),
        compiler_params=params(2),
        name="mix",
    )(*own_lanes(own), other)


def combine(wide, others, masks, bits, factor):
    def kernel(*refs):
        out_refs = refs[1 + len(others) :]
        mixed = None
        for ref, mask in zip(refs, [0] + masks):
            value = ref[...].astype(f32)
            flips = [bit_of("hid", 1 << bit) for bit in bits if not mask >> bit & 1]
            if flips:
                value = jnp.where(sum(flips) % 2 == 1, -value, value)
            mixed = value if mixed is None else mixed + value
        if factor is None:
            out_refs[0][...] = mixed
            out_refs[1][...] = mixed.astype(bf16)
        else:
            out_refs[0][...] = (mixed * factor).astype(bf16)

    types = (f32, bf16) if factor is None else (bf16,)
    return pl.pallas_call(
        kernel,
        out_shape=tuple(jax.ShapeDtypeStruct(wide.shape, t) for t in types),
        in_specs=[VMEM] * (1 + len(others)),
        out_specs=(VMEM,) * len(types),
        compiler_params=params(2),
        name="combine",
    )(wide, *others)


def add(total, arrived, last, estimate):
    def kernel(*refs):
        out_refs = refs[1 + len(arrived) :]
        value = refs[0][...]
        for ref in refs[1 : 1 + len(arrived)]:
            value = value + ref[...].astype(f32)
        if not last:
            out_refs[0][...] = value
        out_refs[-1][...] = value.astype(bf16)

    types = (bf16,) if last else (f32, bf16)
    return pl.pallas_call(
        kernel,
        out_shape=tuple(jax.ShapeDtypeStruct(total.shape, t) for t in types),
        in_specs=[VMEM] * (1 + len(arrived)),
        out_specs=(VMEM,) * len(types),
        compiler_params=params(2, total.shape[0]),
        cost_estimate=estimate,
        name="add",
    )(total, *arrived)


def places(res_rows, own_rows):
    first, me_row = lax.axis_index("hid") * res_rows, lax.axis_index("row")
    found = []
    for r in range(res_rows):
        row = first + r
        found.append(((row // own_rows) ^ me_row) * own_rows + row % own_rows)
    return found


def gather_rows(rows):
    own_rows, depth = rows[0].shape

    def kernel(*refs):
        parts = [ref[...].astype(f32) for ref in refs[:-1]]
        refs[-1][...] = jnp.concatenate(parts, axis=0).astype(bf16)

    return pl.pallas_call(
        kernel,
        out_shape=jax.ShapeDtypeStruct((own_rows * len(rows), depth), bf16),
        in_specs=[VMEM] * len(rows),
        out_specs=VMEM,
        compiler_params=params(2, own_rows * len(rows)),
        name="gather_rows",
    )(*rows)


def down_half(rows, weight, scale, residual, own_rows, other_half, out_type):
    count, depth = rows.shape
    half = weight.shape[1] // 2
    bn = tile_of(half)

    def kernel(x_ref, w_ref, s_ref, r_ref, o_ref):
        side = bit_of("hid", 1)
        if other_half:
            side = 1 - side
        where = places(r_ref.shape[0], own_rows)
        index = lax.broadcasted_iota(jnp.int32, (count, bn), 0)

        for n in range(half // bn):
            there = pl.ds(pl.multiple_of(side * half + n * bn, lanes), bn)
            total = jnp.dot(x_ref[...], w_ref[:, there], preferred_element_type=f32)
            total = total * (s_ref[:, there].astype(f32) * 2.0 ** (-23))
            residual_rows = r_ref[:, there].astype(f32)
            for r, place in enumerate(where):
                total = total + jnp.where(index == place, residual_rows[r : r + 1], 0.0)
            o_ref[:, n * bn : (n + 1) * bn] = total.astype(out_type)

    return pl.pallas_call(
        kernel,
        out_shape=jax.ShapeDtypeStruct((count, half), out_type),
        in_specs=[VMEM] * 4,
        out_specs=VMEM,
        compiler_params=params(14, count),
        cost_estimate=cost(2 * count * depth * half, 2 * depth * half),
        name="down_other" if other_half else "down_own",
    )(rows, weight, scale, residual)


def qkv_half(stream, gain, weight, before, own_rows):
    count, depth = stream.shape
    width = weight.shape[1]
    bn = tile_of(width)
    own_half = before is None
    first_rows = [(0, count)] if own_half else [(0, own_rows), (own_rows, count - own_rows)]

    def kernel(x_ref, g_ref, w_ref, *refs):
        before_ref = None if own_half else refs[0]
        out_refs, scaled = refs[-1 - len(first_rows) : -1], refs[-1]
        side = bit_of("hid", 1)
        if not own_half:
            side = 1 - side
        there = pl.ds(pl.multiple_of(side * depth, depth), depth)
        wide = x_ref[...].astype(f32)
        scaled[...] = (wide * g_ref[:, there].astype(f32)).astype(bf16)
        squares = jnp.broadcast_to(jnp.sum(wide * wide, axis=1, keepdims=True), (count, lanes))

        def put(columns, value):
            if not own_half:
                value = value + before_ref[:, columns]
            for ref, (start, size) in zip(out_refs, first_rows):
                ref[:, columns] = value[start : start + size]

        put(pl.ds(width, lanes), squares)

        for n in range(width // bn):
            columns = pl.ds(n * bn, bn)
            put(columns, jnp.dot(scaled[...], w_ref[there, columns], preferred_element_type=f32))

    operands = (stream, gain, weight) + (() if own_half else (before,))
    return pl.pallas_call(
        kernel,
        out_shape=tuple(jax.ShapeDtypeStruct((size, width + lanes), f32) for _, size in first_rows),
        in_specs=[VMEM] * len(operands),
        out_specs=(VMEM,) * len(first_rows),
        scratch_shapes=[pltpu.VMEM((count, depth), bf16)],
        compiler_params=params(2, count),
        cost_estimate=cost(2 * count * depth * width, 2 * depth * width),
        name="qkv_own" if own_half else "qkv_other",
    )(*operands)


def take_rows(stream, stream_other, res_rows, own_rows):
    count, half = stream.shape

    def kernel(own_ref, other_ref, out_ref):
        index = lax.broadcasted_iota(jnp.int32, (count, half), 0)
        side = bit_of("hid", 1)
        for ref, at in ((own_ref, side), (other_ref, 1 - side)):
            wide = ref[...].astype(f32)
            taken = [
                jnp.sum(jnp.where(index == place, wide, 0.0), axis=0, keepdims=True)
                for place in places(res_rows, own_rows)
            ]
            there = pl.ds(pl.multiple_of(at * half, half), half)
            out_ref[:, there] = jnp.concatenate(taken, axis=0).astype(bf16)

    return pl.pallas_call(
        kernel,
        out_shape=jax.ShapeDtypeStruct((res_rows, 2 * half), bf16),
        in_specs=[VMEM] * 2,
        out_specs=VMEM,
        compiler_params=params(2, count),
        name="take_rows",
    )(stream, stream_other)


def finish(mine, arrived, scales, features):
    rows, wide = mine.shape
    width = wide - lanes

    def kernel(*refs):
        mine_ref, scale_ref, out_ref = refs[0], refs[-2], refs[-1]
        total = mine_ref[...]
        for ref in refs[1:-2]:
            total = total + ref[...]
        inverse = lax.rsqrt(total[:, width : width + 1] / features + epsilon)
        output_scale = scale_ref[...].astype(f32) * 2.0 ** (-22)
        out_ref[...] = (total[:, :width] * inverse * output_scale).astype(bf16)

    return pl.pallas_call(
        kernel,
        out_shape=jax.ShapeDtypeStruct((rows, width), bf16),
        in_specs=[VMEM] * (2 + len(arrived)),
        out_specs=VMEM,
        compiler_params=params(2 * (1 + len(arrived))),
        name="finish",
    )(mine, *arrived, scales)


def body(
    gate_proj,
    up_proj,
    hadamard_signs,
    down_codes,
    down_scales,
    residual,
    norm_gain,
    qkv_codes,
    qkv_scales,
):
    hid, n_row = lax.axis_size("hid"), lax.axis_size("row")
    own_rows, depth = gate_proj.shape
    res_rows, features = residual.shape
    count = hid.bit_length() - 1
    steps = [[0]] + [list(range(b, min(b + 2, count))) for b in range(1, count, 2)]
    partners = [[1 << b[0]] if len(b) == 1 else [1 << b[1], 1 << b[0] | 1 << b[1], 1 << b[0]] for b in steps]

    send = signed_units(gate_proj, up_proj, hadamard_signs)
    for k, (bits, masks) in enumerate(zip(steps, partners)):
        others = [exchange(send, "hid", mask) for mask in masks]
        if k == 0:
            wide, send = mix(send, *others)
        elif k < len(steps) - 1:
            wide, send = combine(wide, others, masks, bits, None)
        else:
            (rotated,) = combine(wide, others, masks, bits, 1.0 / math.sqrt(depth * hid))
    rows = [rotated] + [exchange(rotated, "row", j) for j in range(1, n_row)]
    rows = gather_rows(rows)

    scale = down_scales.reshape(1, -1)
    theirs = down_half(rows, down_codes, scale, residual, own_rows, True, bf16)
    arrived = exchange(theirs, "hid", 1)
    total = down_half(rows, down_codes, scale, residual, own_rows, False, f32)
    arrived = [arrived]
    for k, masks in enumerate(partners[1:]):
        total, send = add(total, arrived, False, cost(100_000_000_000, 0) if k == 0 else None)
        arrived = [exchange(send, "hid", mask) for mask in masks]
    (stream,) = add(total, arrived, True, None)
    stream_other = exchange(stream, "hid", 1)

    gain = norm_gain.reshape(1, -1)
    (part,) = qkv_half(stream, gain, qkv_codes, None, own_rows)
    mine, rest = qkv_half(stream_other, gain, qkv_codes, part, own_rows)
    arrived = [exchange(rest[(j - 1) * own_rows : j * own_rows], "row", j) for j in range(1, n_row)]
    joined_qkv = finish(mine, arrived, qkv_scales.reshape(1, -1), features * n_row)
    return (take_rows(stream, stream_other, res_rows, own_rows), joined_qkv)


def solution(mesh):
    return jax.shard_map(
        body,
        mesh=mesh,
        in_specs=(
            P(("groups", "row"), "hid"),
            P(("groups", "row"), "hid"),
            P("hid"),
            P("hid", "row"),
            P("row"),
            P(("groups", "hid"), "row"),
            P("row"),
            P("row", "hid"),
            P("hid"),
        ),
        out_specs=(P(("groups", "hid"), "row"), P(("groups", "row"), "hid")),
        check_vma=False,
    )
```

```python
import math

import jax
import jax.numpy as jnp
from jax import lax
from jax.experimental import pallas as pl
from jax.experimental.pallas import tpu as pltpu
from jax.sharding import PartitionSpec as P

epsilon = 1e-05
lanes = 128
VMEM = pl.BlockSpec(memory_space=pltpu.VMEM)
HBM = pl.BlockSpec(memory_space=pltpu.HBM)
f32, bf16 = jnp.float32, jnp.bfloat16


def exchange(block, axis, distance):
    count = lax.axis_size(axis)
    return lax.ppermute(block, axis, [(i, i ^ distance) for i in range(count)])


def bit_of(axis, distance):
    return lax.axis_index(axis) // distance % 2


def in_hbm(array):
    return pltpu.with_memory_space_constraint(array, pltpu.HBM)


def in_vmem(array):
    return pltpu.with_memory_space_constraint(array, pltpu.VMEM)


def params(mib, rows=16):
    return pltpu.CompilerParams(vmem_limit_bytes=mib * max(1, rows // 16) << 20)


def cost(flops, nbytes):
    return pl.CostEstimate(flops=flops, bytes_accessed=nbytes, transcendentals=0)


def tile_of(width):
    parts = next(p for p in (1, 2, 3, 4, 6, 8, 9, 12) if width // p <= 2304 and width % (p * lanes) == 0)
    return width // parts


def signed_kernel(gate_hbm, up_hbm, sign_hbm, out_ref, gate_ref, up_ref, sign_ref, sems):
    copies = [
        pltpu.make_async_copy(gate_hbm, gate_ref, sems.at[0]),
        pltpu.make_async_copy(up_hbm, up_ref, sems.at[1]),
        pltpu.make_async_copy(sign_hbm, sign_ref, sems.at[2]),
    ]
    for copy in copies:
        copy.start()
    for copy in copies:
        copy.wait()
    gate = gate_ref[...].astype(f32)
    hidden = (gate / (1.0 + jnp.exp(-gate)) * up_ref[...].astype(f32)).astype(bf16)
    flips = (1 - 2 * sign_ref[...]).astype(f32)
    out_ref[...] = (hidden.astype(f32) * flips).astype(bf16)


def signed_units(gate, up, signs):
    signs = signs.reshape(1, -1)
    return pl.pallas_call(
        signed_kernel,
        out_shape=jax.ShapeDtypeStruct(gate.shape, bf16),
        in_specs=[HBM] * 3,
        out_specs=VMEM,
        scratch_shapes=[
            pltpu.VMEM(gate.shape, bf16),
            pltpu.VMEM(gate.shape, bf16),
            pltpu.VMEM(signs.shape, jnp.int32),
            pltpu.SemaphoreType.DMA((3,)),
        ],
        compiler_params=params(2),
        cost_estimate=cost(40_000_000_000, 0),
        name="signed_units",
    )(in_hbm(gate), in_hbm(up), in_hbm(signs))


def hadamard_128():
    both = lax.broadcasted_iota(jnp.int32, (lanes, lanes), 0) & lax.broadcasted_iota(
        jnp.int32, (lanes, lanes), 1
    )
    for shift in (4, 2, 1):
        both = both ^ (both >> shift)
    return (1 - 2 * (both & 1)).astype(f32).astype(bf16)


def lane_blocks(ref, matrix):
    rows, width = ref.shape
    wide = ref[...].astype(f32)
    blocks = [wide[:, j * lanes : (j + 1) * lanes] for j in range(width // lanes)]
    tall = jnp.concatenate(blocks, axis=0).astype(bf16)
    product = jnp.dot(tall, matrix, preferred_element_type=f32)
    return [product[j * rows : (j + 1) * rows] for j in range(len(blocks))]


def own_lanes(own):
    def kernel(own_ref, mixed_ref, matrix_ref):
        matrix = hadamard_128()
        matrix_ref[...] = matrix
        sign = (1 - 2 * bit_of("hid", 1)).astype(f32)
        for j, block in enumerate(lane_blocks(own_ref, matrix)):
            mixed_ref[:, j * lanes : (j + 1) * lanes] = block * sign

    return pl.pallas_call(
        kernel,
        out_shape=(jax.ShapeDtypeStruct(own.shape, f32), jax.ShapeDtypeStruct((lanes, lanes), bf16)),
        in_specs=[VMEM],
        out_specs=(VMEM, VMEM),
        compiler_params=params(2),
        name="own_lanes",
    )(own)


def mix(own, other):
    def kernel(mixed_ref, matrix_ref, other_ref, wide_ref, send_ref):
        blocks = [
            block + mixed_ref[:, j * lanes : (j + 1) * lanes]
            for j, block in enumerate(lane_blocks(other_ref, matrix_ref[...]))
        ]
        step = 1
        while step < len(blocks):
            for j in range(len(blocks)):
                if not j & step:
                    a, b = blocks[j], blocks[j | step]
                    blocks[j], blocks[j | step] = a + b, a - b
            step *= 2
        for j, block in enumerate(blocks):
            wide_ref[:, j * lanes : (j + 1) * lanes] = block
            send_ref[:, j * lanes : (j + 1) * lanes] = block.astype(bf16)

    return pl.pallas_call(
        kernel,
        out_shape=(jax.ShapeDtypeStruct(other.shape, f32), jax.ShapeDtypeStruct(other.shape, bf16)),
        in_specs=[VMEM] * 3,
        out_specs=(VMEM, VMEM),
        compiler_params=params(2),
        name="mix",
    )(*own_lanes(own), other)


def combine(wide, others, masks, bits, factor):
    def kernel(*refs):
        out_refs = refs[1 + len(others) :]
        mixed = None
        for ref, mask in zip(refs, [0] + masks):
            value = ref[...].astype(f32)
            flips = [bit_of("hid", 1 << bit) for bit in bits if not mask >> bit & 1]
            if flips:
                value = jnp.where(sum(flips) % 2 == 1, -value, value)
            mixed = value if mixed is None else mixed + value
        if factor is None:
            out_refs[0][...] = mixed
            out_refs[1][...] = mixed.astype(bf16)
        else:
            out_refs[0][...] = (mixed * factor).astype(bf16)

    types = (f32, bf16) if factor is None else (bf16,)
    return pl.pallas_call(
        kernel,
        out_shape=tuple(jax.ShapeDtypeStruct(wide.shape, t) for t in types),
        in_specs=[VMEM] * (1 + len(others)),
        out_specs=(VMEM,) * len(types),
        compiler_params=params(2),
        name="combine",
    )(wide, *others)


def add(total, arrived, last, estimate):
    def kernel(*refs):
        out_refs = refs[1 + len(arrived) :]
        value = refs[0][...]
        for ref in refs[1 : 1 + len(arrived)]:
            value = value + ref[...].astype(f32)
        if not last:
            out_refs[0][...] = value
        out_refs[-1][...] = value.astype(bf16)

    types = (bf16,) if last else (f32, bf16)
    return pl.pallas_call(
        kernel,
        out_shape=tuple(jax.ShapeDtypeStruct(total.shape, t) for t in types),
        in_specs=[VMEM] * (1 + len(arrived)),
        out_specs=(VMEM,) * len(types),
        compiler_params=params(2, total.shape[0]),
        cost_estimate=estimate,
        name="add",
    )(total, *arrived)


def places(res_rows, own_rows):
    first, me_row = lax.axis_index("hid") * res_rows, lax.axis_index("row")
    found = []
    for r in range(res_rows):
        row = first + r
        found.append(((row // own_rows) ^ me_row) * own_rows + row % own_rows)
    return found


def gather_rows(rows):
    own_rows, depth = rows[0].shape

    def kernel(*refs):
        parts = [ref[...].astype(f32) for ref in refs[:-1]]
        refs[-1][...] = jnp.concatenate(parts, axis=0).astype(bf16)

    return pl.pallas_call(
        kernel,
        out_shape=jax.ShapeDtypeStruct((own_rows * len(rows), depth), bf16),
        in_specs=[VMEM] * len(rows),
        out_specs=VMEM,
        compiler_params=params(2, own_rows * len(rows)),
        name="gather_rows",
    )(*rows)


def down_half(rows, weight, scale, residual, own_rows, other_half, out_type):
    count, depth = rows.shape
    half = weight.shape[1] // 2
    bn = half // 2

    def kernel(x_ref, w_ref, s_ref, r_ref, o_ref):
        side = bit_of("hid", 1)
        if other_half:
            side = 1 - side
        where = places(r_ref.shape[0], own_rows)
        index = lax.broadcasted_iota(jnp.int32, (count, bn), 0)

        for n in range(half // bn):
            there = pl.ds(pl.multiple_of(side * half + n * bn, lanes), bn)
            total = jnp.dot(x_ref[...], w_ref[:, there], preferred_element_type=f32)
            total = total * (s_ref[:, there].astype(f32) * 2.0 ** (-23))
            residual_rows = r_ref[:, there].astype(f32)
            for r, place in enumerate(where):
                total = total + jnp.where(index == place, residual_rows[r : r + 1], 0.0)
            o_ref[:, n * bn : (n + 1) * bn] = total.astype(out_type)

    return pl.pallas_call(
        kernel,
        out_shape=jax.ShapeDtypeStruct((count, half), out_type),
        in_specs=[VMEM] * 4,
        out_specs=VMEM,
        compiler_params=params(14, count),
        cost_estimate=cost(2 * count * depth * half, 2 * depth * half),
        name="down_other" if other_half else "down_own",
    )(rows, weight, scale, residual)


def qkv_half(stream, gain, weight, before, own_rows):
    count, depth = stream.shape
    width = weight.shape[1]
    bn = tile_of(width)
    own_half = before is None
    first_rows = [(0, count)] if own_half else [(0, own_rows), (own_rows, count - own_rows)]

    def kernel(x_ref, g_ref, w_ref, *refs):
        before_ref = None if own_half else refs[0]
        out_refs, scaled = refs[-1 - len(first_rows) : -1], refs[-1]
        side = bit_of("hid", 1)
        if not own_half:
            side = 1 - side
        there = pl.ds(pl.multiple_of(side * depth, depth), depth)
        wide = x_ref[...].astype(f32)
        scaled[...] = (wide * g_ref[:, there].astype(f32)).astype(bf16)
        squares = jnp.broadcast_to(jnp.sum(wide * wide, axis=1, keepdims=True), (count, lanes))

        def put(columns, value):
            if not own_half:
                value = value + before_ref[:, columns]
            for ref, (start, size) in zip(out_refs, first_rows):
                ref[:, columns] = value[start : start + size]

        put(pl.ds(width, lanes), squares)

        for n in range(width // bn):
            columns = pl.ds(n * bn, bn)
            put(columns, jnp.dot(scaled[...], w_ref[there, columns], preferred_element_type=f32))

    operands = (stream, gain, weight) + (() if own_half else (before,))
    return pl.pallas_call(
        kernel,
        out_shape=tuple(jax.ShapeDtypeStruct((size, width + lanes), f32) for _, size in first_rows),
        in_specs=[VMEM] * len(operands),
        out_specs=(VMEM,) * len(first_rows),
        scratch_shapes=[pltpu.VMEM((count, depth), bf16)],
        compiler_params=params(2, count),
        cost_estimate=cost(2 * count * depth * width, 2 * depth * width),
        name="qkv_own" if own_half else "qkv_other",
    )(*operands)


def take_rows(stream, stream_other, res_rows, own_rows):
    count, half = stream.shape

    def kernel(own_ref, other_ref, out_ref):
        index = lax.broadcasted_iota(jnp.int32, (count, half), 0)
        side = bit_of("hid", 1)
        for ref, at in ((own_ref, side), (other_ref, 1 - side)):
            wide = ref[...].astype(f32)
            taken = [
                jnp.sum(jnp.where(index == place, wide, 0.0), axis=0, keepdims=True)
                for place in places(res_rows, own_rows)
            ]
            there = pl.ds(pl.multiple_of(at * half, half), half)
            out_ref[:, there] = jnp.concatenate(taken, axis=0).astype(bf16)

    return pl.pallas_call(
        kernel,
        out_shape=jax.ShapeDtypeStruct((res_rows, 2 * half), bf16),
        in_specs=[VMEM] * 2,
        out_specs=VMEM,
        compiler_params=params(2, count),
        name="take_rows",
    )(stream, stream_other)


def finish(mine, arrived, scales, features):
    rows, wide = mine.shape
    width = wide - lanes

    def kernel(*refs):
        mine_ref, scale_ref, out_ref = refs[0], refs[-2], refs[-1]
        total = mine_ref[...]
        for ref in refs[1:-2]:
            total = total + ref[...]
        inverse = lax.rsqrt(total[:, width : width + 1] / features + epsilon)
        output_scale = scale_ref[...].astype(f32) * 2.0 ** (-22)
        out_ref[...] = (total[:, :width] * inverse * output_scale).astype(bf16)

    return pl.pallas_call(
        kernel,
        out_shape=jax.ShapeDtypeStruct((rows, width), bf16),
        in_specs=[VMEM] * (2 + len(arrived)),
        out_specs=VMEM,
        compiler_params=params(2 * (1 + len(arrived))),
        name="finish",
    )(mine, *arrived, scales)


def body(
    gate_proj,
    up_proj,
    hadamard_signs,
    down_codes,
    down_scales,
    residual,
    norm_gain,
    qkv_codes,
    qkv_scales,
):
    hid, n_row = lax.axis_size("hid"), lax.axis_size("row")
    own_rows, depth = gate_proj.shape
    res_rows, features = residual.shape
    count = hid.bit_length() - 1
    steps = [[0]] + [list(range(b, min(b + 2, count))) for b in range(1, count, 2)]
    partners = [[1 << b[0]] if len(b) == 1 else [1 << b[1], 1 << b[0] | 1 << b[1], 1 << b[0]] for b in steps]

    send = signed_units(gate_proj, up_proj, hadamard_signs)
    for k, (bits, masks) in enumerate(zip(steps, partners)):
        others = [exchange(send, "hid", mask) for mask in masks]
        if k == 0:
            wide, send = mix(send, *others)
        elif k < len(steps) - 1:
            wide, send = combine(wide, others, masks, bits, None)
        else:
            (rotated,) = combine(wide, others, masks, bits, 1.0 / math.sqrt(depth * hid))
    rows = [rotated] + [exchange(rotated, "row", j) for j in range(1, n_row)]
    rows = gather_rows(rows)

    scale = down_scales.reshape(1, -1)
    theirs = down_half(rows, down_codes, scale, residual, own_rows, True, bf16)
    arrived = exchange(theirs, "hid", 1)
    total = down_half(rows, down_codes, scale, residual, own_rows, False, f32)
    arrived = [arrived]
    for k, masks in enumerate(partners[1:]):
        total, send = add(total, arrived, False, cost(100_000_000_000, 0) if k == 0 else None)
        arrived = [exchange(send, "hid", mask) for mask in masks]
    (stream,) = add(total, arrived, True, None)
    stream_other = exchange(stream, "hid", 1)

    gain = norm_gain.reshape(1, -1)
    (part,) = qkv_half(stream, gain, qkv_codes, None, own_rows)
    mine, rest = qkv_half(stream_other, gain, qkv_codes, part, own_rows)
    arrived = [exchange(rest[(j - 1) * own_rows : j * own_rows], "row", j) for j in range(1, n_row)]
    joined_qkv = finish(mine, arrived, qkv_scales.reshape(1, -1), features * n_row)
    return (take_rows(stream, stream_other, res_rows, own_rows), joined_qkv)


def solution(mesh):
    return jax.shard_map(
        body,
        mesh=mesh,
        in_specs=(
            P(("groups", "row"), "hid"),
            P(("groups", "row"), "hid"),
            P("hid"),
            P("hid", "row"),
            P("row"),
            P(("groups", "hid"), "row"),
            P("row"),
            P("row", "hid"),
            P("hid"),
        ),
        out_specs=(P(("groups", "hid"), "row"), P(("groups", "row"), "hid")),
        check_vma=False,
    )
```
